32 devices in a mesh: items: 4 (over y, x), seq: 8 (over z, core).
Axes of the slice: x: 2, y: 2, z: 4, core: 2. Of those that a mesh axis runs over, the one named last changes fastest.
Arguments:
- tokens: bfloat16 [4, 2048, 1024], P('items', 'seq'), may hold values from -6 to 6
- decay_rate: float32 [8], replicated, may hold values from 0.96 to 1, as said below
- query_weight: bfloat16 [1024, 1024], P(('items', 'seq')), may hold values from -0.1875 to 0.1875
- key_weight: bfloat16 [1024, 1024], P(('items', 'seq')), may hold values from -0.1875 to 0.1875
- value_weight: bfloat16 [1024, 1024], P(('items', 'seq')), may hold values from -0.1875 to 0.1875
- update_weight: bfloat16 [1024, 1024], P(('items', 'seq')), may hold values from -0.1875 to 0.1875
- output_weight: bfloat16 [1024, 1024], P(('items', 'seq')), may hold values from -0.1875 to 0.1875
- gate_weight: bfloat16 [1024, 2816], P(('items', 'seq')), may hold values from -0.1875 to 0.1875
- up_weight: bfloat16 [1024, 2816], P(('items', 'seq')), may hold values from -0.1875 to 0.1875
- down_weight: bfloat16 [2816, 1024], P(None, ('items', 'seq')), may hold values from -0.109375 to 0.109375
- cotangent: bfloat16 [4, 2048, 1024], P('items', 'seq'), may hold values from -6 to 6
Outputs:
- mixed: bfloat16 [4, 2048, 1024], P('items', 'seq')
- tokens_grad: float32 [4, 2048, 1024], P('items', 'seq')
- query_grad: float32 [1024, 1024], P(('items', 'seq'))
- key_grad: float32 [1024, 1024], P(('items', 'seq'))
- value_grad: float32 [1024, 1024], P(('items', 'seq'))
- update_grad: float32 [1024, 1024], P(('items', 'seq'))
- output_grad: float32 [1024, 1024], P(('items', 'seq'))
- gate_grad: float32 [1024, 2816], P(('items', 'seq'))
- up_grad: float32 [1024, 2816], P(('items', 'seq'))
- down_grad: float32 [2816, 1024], P(None, ('items', 'seq'))
The draws below stay inside these ranges and needn't reach their ends.
Inputs may be any that keep to these rules, and one draw needn't show every extreme that they name: decay_rate[h] is lambda_h, the factor by which head h keeps its state from one position to the next.
All inputs are finite; a program needn't handle non-finite values.
Results may differ from the reference program's by a relative error of at most 0.015.
Values may be sent and summed in bfloat16 or wider, within the bound.
No kernel may reach another device: no remote copies, remote signals or barrier semaphores. Data moves between devices by JAX's collectives and lax.ppermute only.
A program may use at most 320 MiB of HBM per device.

```python
import math
import jax
import jax.numpy as jnp
from jax import lax

D = 1024
H = 8
E = 128
FF = 2816
TOK_DEV = 256
LEN = 2048
BATCH = 4


def draw_decay_rate(key, part):
    order = jax.random.permutation(jax.random.fold_in(key, 11), H)
    spread = jax.random.uniform(jax.random.fold_in(key, 12), (H,), jnp.float32)
    slow_heads = order < H // 2
    short_end = 0.5 * LEN
    long_end = 4.0 * LEN
    slow_len = jnp.exp(math.log(short_end) + spread * (math.log(long_end) - math.log(short_end)))
    fast_len = jnp.exp(math.log(30.0) + spread * (math.log(50.0) - math.log(30.0)))
    memory = jnp.where(slow_heads, slow_len, fast_len)
    return jnp.exp(-1.0 / memory)


def shard_levels(own_key, shape, split, smallest, largest):
    factor_of = 1.0
    for dim, shards_of in split:
        heights = jax.random.uniform(jax.random.fold_in(jax.random.fold_in(own_key, 6), dim), (shards_of,), jnp.float32, smallest / len(split), largest / len(split))
        factor_of = factor_of * jnp.repeat(jnp.exp(heights), shape[dim] // shards_of).reshape((-1,) + (1,) * (len(shape) - 1 - dim))
    return factor_of


def normal_values(stream_key, extent, scale, reach, cuts=(), kind=jnp.bfloat16):
    factor_of = shard_levels(stream_key, extent, cuts, -0.22, 0.18) if cuts else 1.0
    result = jax.random.normal(stream_key, extent, jnp.float32) * scale * factor_of
    return jnp.minimum(jnp.maximum(result, -reach), reach).astype(kind)


def setup_inputs(seed: int = 0) -> dict:
    seeds = jax.random.split(jax.random.key(seed), 12)
    return {
        "tokens": normal_values(seeds[0], (BATCH, LEN, D), 1.0, 6.0, ((0, 4), (1, 8))),
        "decay_rate": draw_decay_rate(jax.random.fold_in(seeds[11], 71), 0),
        "query_weight": normal_values(seeds[2], (D, D), D ** -0.5, 0.1875, ((0, 32),)),
        "key_weight": normal_values(seeds[3], (D, D), D ** -0.5, 0.1875, ((0, 32),)),
        "value_weight": normal_values(seeds[4], (D, D), D ** -0.5, 0.1875, ((0, 32),)),
        "update_weight": normal_values(seeds[5], (D, D), D ** -0.5, 0.1875, ((0, 32),)),
        "output_weight": normal_values(seeds[6], (D, D), D ** -0.5, 0.1875, ((0, 32),)),
        "gate_weight": normal_values(seeds[7], (D, FF), D ** -0.5, 0.1875, ((0, 32),)),
        "up_weight": normal_values(seeds[8], (D, FF), D ** -0.5, 0.1875, ((0, 32),)),
        "down_weight": normal_values(seeds[9], (FF, D), FF ** -0.5, 0.109375, ((1, 32),)),
        "cotangent": normal_values(seeds[10], (BATCH, LEN, D), 1.0, 6.0, ((0, 4), (1, 8))),
    }


epsilon = 1e-06
highest = lax.Precision.HIGHEST

@jax.custom_vjp
def low(v):
    return lax.optimization_barrier(v.astype(jnp.bfloat16)).astype(jnp.float32)

@jax.custom_vjp
def low_back(v):
    return v

def low_keep(v):
    return (low(v), None)

def low_pass(kept, grad):
    return (grad,)

def back_keep(v):
    return (v, None)

def back_low(kept, grad):
    return (low(grad),)
low.defvjp(low_keep, low_pass)
low_back.defvjp(back_keep, back_low)

def matmul(left_op, right_op):
    return jnp.dot(left_op, right_op, precision=highest, preferred_element_type=jnp.float32)

def simple_norm(values_in):
    return values_in * lax.rsqrt(lax.optimization_barrier(jnp.mean(values_in * values_in, axis=-1, keepdims=True)) + epsilon)

def swish(values_in):
    return values_in * jax.nn.sigmoid(values_in)

def rotation_tables(positions, head_size):
    half_width = head_size // 2
    pair_index = jnp.arange(half_width, dtype=jnp.int32)
    step_sizes = jnp.right_shift(jnp.full((half_width,), 8192, jnp.int32), pair_index // 5)
    phase_int = positions[:, None] * step_sizes[None, :] % 65536
    angles = phase_int.astype(jnp.float32) * (2.0 * math.pi / 65536.0)
    return (jnp.cos(angles), jnp.sin(angles))

def rotate(values_in, cosine, sine_tab):
    half_width = values_in.shape[-1] // 2
    first_half = values_in[..., :half_width]
    second_half = values_in[..., half_width:]
    wide_cos = cosine[:, None, :]
    wide_sin = sine_tab[:, None, :]
    return jnp.concatenate([first_half * wide_cos - second_half * wide_sin, first_half * wide_sin + second_half * wide_cos], axis=-1)

def layer(seq_tokens, weights, log_decay):
    query_w, key_w, value_w, update_w, output_w, gate_w, up_w, down_w = weights
    length = seq_tokens.shape[0]
    blocks = length // TOK_DEV
    normed_in = low(simple_norm(seq_tokens))
    query_pre = low_back(matmul(normed_in, query_w))
    key_pre = low_back(matmul(normed_in, key_w))
    value_low = low(low_back(matmul(normed_in, value_w)))
    update = low_back(matmul(normed_in, update_w)).reshape(length, H, E)
    positions = jnp.arange(length, dtype=jnp.int32)
    cosine, sine_tab = rotation_tables(positions, E)
    query_act = rotate(swish(query_pre).reshape(length, H, E), cosine, sine_tab)
    key_act = rotate(swish(key_pre).reshape(length, H, E), cosine, sine_tab)
    local_pos = jnp.arange(TOK_DEV).astype(jnp.float32)
    query_decay = jnp.exp(log_decay[None, :] * (local_pos[:, None] + 1.0))
    key_decay = jnp.exp(log_decay[None, :] * (TOK_DEV - 1.0 - local_pos[:, None]))
    offset = local_pos[:, None] - local_pos[None, :]
    decay_mask = jnp.where(offset >= 0.0, jnp.exp(log_decay[:, None, None] * jnp.maximum(offset, 0.0)[None]), 0.0)
    block_shape = (blocks, TOK_DEV, H, E)
    query_blocks = low(query_act).reshape(block_shape)
    key_blocks = low(key_act).reshape(block_shape)
    value_blocks = value_low.reshape(block_shape)
    query_scaled = low(query_act.reshape(block_shape) * query_decay[None, :, :, None])
    key_scaled = low(key_act.reshape(block_shape) * key_decay[None, :, :, None])

    def intra_block(operands):
        query_b, key_b, value_b = operands
        scores = low_back(jnp.einsum('the,she->hts', query_b, key_b, precision=highest))
        weight_b = low(scores * decay_mask)
        return jnp.einsum('hts,she->the', weight_b, value_b, precision=highest)
    intra = lax.map(jax.checkpoint(intra_block), (query_blocks, key_blocks, value_blocks))
    local_states = low_back(jnp.einsum('bshe,bshf->bhef', key_scaled, value_blocks, precision=highest))
    factor = jnp.exp(log_decay * TOK_DEV)

    def advance(carry, state_in):
        return (factor[:, None, None] * carry + state_in, carry)
    _, prefix = lax.scan(advance, jnp.zeros((H, E, E), jnp.float32), local_states)
    inter = jnp.einsum('bthe,bhef->bthf', query_scaled, low(prefix), precision=highest)
    attn_raw = low_back((intra + inter).reshape(length, H, E))
    mixed_in = low((simple_norm(attn_raw) * update).reshape(length, D))
    attn_out = low_back(matmul(mixed_in, output_w))
    resid = seq_tokens + attn_out
    normed_mid = low(simple_norm(resid))
    gate_act = low_back(matmul(normed_mid, gate_w))
    up_act = low_back(matmul(normed_mid, up_w))
    hidden = low(gate_act * up_act)
    ffn_out = low_back(matmul(hidden, down_w))
    return resid + ffn_out

def reference(tokens, decay_rate, query_weight, key_weight, value_weight, update_weight, output_weight, gate_weight, up_weight, down_weight, cotangent):
    weights = tuple((weight.astype(jnp.float32) for weight in (query_weight, key_weight, value_weight, update_weight, output_weight, gate_weight, up_weight, down_weight)))
    log_decay = jnp.log(decay_rate)

    def forward(seq_tokens, weight_set):
        return layer(seq_tokens, weight_set, log_decay)

    def one_sequence(totals, operands):
        seq_tokens, seq_cot = operands
        output, pullback = jax.vjp(forward, seq_tokens.astype(jnp.float32), weights)
        token_grad, weight_grads = pullback(seq_cot.astype(jnp.float32))
        totals = tuple((total + addend for total, addend in zip(totals, weight_grads)))
        return (totals, (output.astype(jnp.bfloat16), token_grad))
    zero_sums = tuple((jnp.zeros_like(weight) for weight in weights))
    totals, outputs = lax.scan(one_sequence, zero_sums, (tokens, cotangent))
    mixed, tokens_grad = outputs
    return (mixed, tokens_grad, totals[0], totals[1], totals[2], totals[3], totals[4], totals[5], totals[6], totals[7])
```

```python
import math

import jax
import jax.numpy as jnp
from jax import lax
from jax.sharding import PartitionSpec as P

epsilon = 1e-06
AXES = ("items", "seq")
f32 = jnp.float32
bf16 = jnp.bfloat16


def mm(a, b):
    return jnp.dot(a, b, preferred_element_type=f32)


def mm_tn(a, b):
    return lax.dot_general(a, b, (((0,), (0,)), ((), ())), preferred_element_type=f32)


def mm_nt(a, b):
    return lax.dot_general(a, b, (((1,), (1,)), ((), ())), preferred_element_type=f32)


def norm_factor(v):
    return lax.rsqrt(jnp.mean(v * v, axis=-1, keepdims=True) + epsilon)


def norm_back(normed, scale, grad):
    return scale * (grad - normed * jnp.mean(grad * normed, axis=-1, keepdims=True))


def pick(bit, a, b):
    return jnp.where(bit == 0, a, b)


def order(bit, own, other, axis):
    return jnp.where(
        bit == 0, jnp.concatenate([own, other], axis), jnp.concatenate([other, own], axis)
    )


class Place:
    def __init__(self, items, seqs):
        self.items, self.seqs, self.groups = items, seqs, seqs // 4
        self.count = items * seqs
        self.item = lax.axis_index("items")
        where = lax.axis_index("seq")
        self.core, self.pair, self.group = where % 2, (where // 2) % 2, where // 4
        self.member = where % 4

    def swap(self, v, mask):
        return lax.ppermute(v, AXES, [(d, d ^ mask) for d in range(self.count)])

    def core_swap(self, v):
        return self.swap(v, 1)

    def pair_swap(self, v):
        return self.swap(v, 2)

    def group_swap(self, v, k):
        return self.swap(v, 4 * k)

    def item_swap(self, v, k):
        return self.swap(v, self.seqs * k)

    def group_shift(self, v, k):
        pairs = []
        for d in range(self.count):
            g = (d % self.seqs) // 4 + k
            if 0 <= g < self.groups:
                pairs.append((d, d + 4 * k))
        return lax.ppermute(v, AXES, pairs)

    def spread(self, v):
        v = v[None]
        v = order(self.pair, v, self.pair_swap(v), 0)[:, None]
        return order(self.core, v, self.core_swap(v), 1)

    def collect(self, v):
        keep, send = pick(self.core, v[:, 0], v[:, 1]), pick(self.core, v[:, 1], v[:, 0])
        v = keep + self.core_swap(send.astype(bf16)).astype(f32)
        keep, send = pick(self.pair, v[0], v[1]), pick(self.pair, v[1], v[0])
        return keep + self.pair_swap(send.astype(bf16)).astype(f32)

    def exchange(self, v):
        keep, send = pick(self.core, v[:, 0], v[:, 1]), pick(self.core, v[:, 1], v[:, 0])
        v = order(self.core, keep[:, None], self.core_swap(send)[:, None], 1)
        keep, send = pick(self.pair, v[0], v[1]), pick(self.pair, v[1], v[0])
        return order(self.pair, keep[None], self.pair_swap(send)[None], 0)

    def permute(self, v):
        rows, width = v.shape
        block = width // (self.items * self.groups)
        v = v.reshape(rows, self.items, self.groups, block)
        for axis, size, here in ((1, self.items, self.item), (2, self.groups, self.group)):
            bit = 1
            while bit < size:
                shape = v.shape
                w = v.reshape(shape[:axis] + (size // (2 * bit), 2, bit) + shape[axis + 1 :])
                w = pick((here // bit) % 2, w, jnp.flip(w, axis + 1))
                v = w.reshape(shape)
                bit *= 2
        return v.reshape(rows, width)


def by_member(w, pad):
    rows, width = w.shape
    w = w.reshape(rows, 4, width // 4).transpose(1, 0, 2)
    return jnp.pad(w, ((0, 0), (0, 0), (0, pad))) if pad else w


def gather_weights(at, raw):
    v = raw.reshape((2, 2) + raw.shape[1:])
    v = at.exchange(v).reshape(-1, raw.shape[2])
    pieces = [v] + [at.group_swap(v, k) for k in range(1, at.groups)]
    half = max(1, at.groups // 2)
    table = {}
    for k, piece in enumerate(pieces):
        one, two = (1, 2) if k < half else (2, 1)
        first = at.item_swap(piece, one)
        second = at.item_swap(piece, two)
        table[0, k], table[one, k], table[two, k] = piece, first, second
        table[3, k] = at.item_swap(first, two)
    return jnp.concatenate(
        [table[i, k] for i in range(at.items) for k in range(at.groups)], axis=0
    )


def scatter_grads(at, grad):
    width = grad.shape[1]
    low = grad.reshape(at.items, at.groups, -1, width)
    half = max(1, at.groups // 2)
    sums = []
    for part, one, two in ((slice(0, half), 1, 2), (slice(half, at.groups), 2, 1)):
        v = low[:, part]
        if v.shape[1] == 0:
            continue
        got = at.item_swap(jnp.stack([v[one], v[3]]).astype(bf16), one).astype(f32)
        got2 = at.item_swap((v[two] + got[1]).astype(bf16), two).astype(f32)
        sums.append(v[0] + got[0] + got2)
    v = jnp.concatenate(sums, axis=0)
    total = v[0]
    for k in range(1, at.groups):
        total = total + at.group_swap(v[k].astype(bf16), k).astype(f32)
    total = total.reshape(2, 2, -1, width)
    keep, send = pick(at.pair, total[0], total[1]), pick(at.pair, total[1], total[0])
    got = at.pair_swap(send.astype(bf16)).astype(f32)
    v = order(at.pair, keep[None], got[None], 0)
    keep, send = pick(at.core, v[:, 0], v[:, 1]), pick(at.core, v[:, 1], v[:, 0])
    got = at.core_swap(send.astype(bf16)).astype(f32)
    v = order(at.core, keep[:, None], got[:, None], 1)
    return v.reshape(4, -1, width).transpose(1, 0, 2)


def rotation_tables(positions, head_size):
    half_width = head_size // 2
    pair_index = jnp.arange(half_width, dtype=jnp.int32)
    step_sizes = jnp.right_shift(jnp.full((half_width,), 8192, jnp.int32), pair_index // 5)
    phase_int = positions[:, None] * step_sizes[None, :] % 65536
    angles = phase_int.astype(f32) * (2.0 * math.pi / 65536.0)
    return (jnp.cos(angles), jnp.sin(angles))


def rotate(v, cosine, sine):
    half = v.shape[-1] // 2
    a, b = v[..., :half], v[..., half:]
    return jnp.concatenate([a * cosine - b * sine, a * sine + b * cosine], axis=-1)


def ein(spec, a, b):
    return jnp.einsum(spec, a, b, preferred_element_type=f32)


def make_body(items, seqs):
    def body(
        tokens,
        decay_rate,
        query_weight,
        key_weight,
        value_weight,
        update_weight,
        output_weight,
        gate_weight,
        up_weight,
        down_weight,
        cotangent,
    ):
        at = Place(items, seqs)
        width = tokens.shape[-1]
        rows = tokens.shape[1]
        heads = decay_rate.shape[0]
        size = width // heads
        own_heads = heads // 4
        own_width = width // 4
        hidden = gate_weight.shape[1] // 4
        pad = -hidden % 256
        wide = hidden + pad

        attn_raw = jnp.concatenate(
            [by_member(w, 0) for w in (query_weight, key_weight, value_weight, update_weight)], 2
        )
        ffn_raw = jnp.concatenate(
            [by_member(w, pad) for w in (gate_weight, up_weight, down_weight.T)]
            + [by_member(output_weight, 0)],
            2,
        )
        attn_w = gather_weights(at, attn_raw)
        ffn_w = gather_weights(at, ffn_raw)
        gate_w, up_w, down_w, out_part = (
            ffn_w[:, :wide],
            ffn_w[:, wide : 2 * wide],
            ffn_w[:, 2 * wide : 3 * wide],
            ffn_w[:, 3 * wide :],
        )
        out_w = at.spread(out_part).reshape(4, width, own_width).transpose(1, 0, 2)
        out_w = out_w.reshape(width, width)

        inputs = tokens.reshape(rows, width).astype(f32)
        scale_in = norm_factor(inputs)
        normed_in = inputs * scale_in
        h1 = at.spread(at.permute(normed_in.astype(bf16))).reshape(4 * rows, width)
        grad_ffn = cotangent.reshape(rows, width)
        cot = at.spread(at.permute(grad_ffn)).reshape(4 * rows, width)

        pre = mm(h1, attn_w).reshape(4, rows, 4, own_heads, size).transpose(2, 0, 3, 1, 4)
        query_pre, key_pre, update = pre[0], pre[1], pre[3]
        values = pre[2].astype(bf16)

        start = at.group * 4 * rows
        positions = start + jnp.arange(4 * rows, dtype=jnp.int32)
        cosine, sine = rotation_tables(positions, size)
        cosine, sine = (t.reshape(4, 1, rows, -1) for t in (cosine, sine))
        query_sig, key_sig = jax.nn.sigmoid(query_pre), jax.nn.sigmoid(key_pre)
        query_act = rotate(query_pre * query_sig, cosine, sine)
        key_act = rotate(key_pre * key_sig, cosine, sine)
        log_decay = lax.dynamic_slice(jnp.log(decay_rate), (at.member * own_heads,), (own_heads,))
        local = jnp.arange(rows).astype(f32)
        ld = log_decay[:, None]
        query_decay = jnp.exp(ld * (local + 1.0))[:, :, None]
        key_decay = jnp.exp(ld * (rows - 1.0 - local))[:, :, None]
        offset = local[:, None] - local[None, :]
        mask = jnp.where(
            offset >= 0.0, jnp.exp(log_decay[:, None, None] * jnp.maximum(offset, 0.0)), 0.0
        )
        queries, keys = query_act.astype(bf16), key_act.astype(bf16)
        query_scaled = (query_act * query_decay).astype(bf16)
        key_scaled = (key_act * key_decay).astype(bf16)
        factor = jnp.exp(log_decay * rows)[:, None, None]
        far = jnp.exp(log_decay * (4.0 * rows))[:, None, None]

        states = ein("bhse,bhsf->bhef", key_scaled, values)
        prefix = [jnp.zeros_like(states[0])]
        for b in range(4):
            prefix.append(factor * prefix[b] + states[b])
        before = jnp.zeros_like(states[0])
        weight = jnp.ones_like(far)
        for k in range(1, at.groups):
            before = before + weight * at.group_shift(prefix[4], k)
            weight = weight * far
        scores = ein("bhte,bhse->bhts", queries, keys)
        weight_low = (scores * mask).astype(bf16)
        intra = ein("bhts,bhse->bhte", weight_low, values)
        full = []
        weight = jnp.ones_like(factor)
        for b in range(4):
            full.append(prefix[b] + weight * before)
            weight = weight * factor
        prefix_low = jnp.stack(full).astype(bf16)
        attn = intra + ein("bhte,bhef->bhtf", query_scaled, prefix_low)
        scale_heads = norm_factor(attn)
        normed_heads = attn * scale_heads
        mixed_low = (normed_heads * update).astype(bf16)
        own = at.exchange(mixed_low.reshape((2, 2) + mixed_low.shape[1:]))
        own = own.reshape(heads, rows, size).transpose(1, 0, 2).reshape(rows, width)
        own = at.permute(own)
        resid = inputs + mm(own, out_w)
        scale_mid = norm_factor(resid)
        normed_mid = resid * scale_mid
        h2 = at.spread(at.permute(normed_mid.astype(bf16))).reshape(4 * rows, width)
        gate_act, up_act = mm(h2, gate_w), mm(h2, up_w)
        grad_hidden = mm(cot, down_w)
        hidden_low = (gate_act * up_act).astype(bf16)
        grad_gate = (grad_hidden * up_act).astype(bf16)
        grad_up = (grad_hidden * gate_act).astype(bf16)
        grad_mid = mm_nt(grad_gate, gate_w) + mm_nt(grad_up, up_w)
        grad_mid = at.permute(at.collect(grad_mid.reshape(2, 2, rows, width)))
        ffn_grads = jnp.concatenate(
            [mm_tn(h2, grad_gate), mm_tn(h2, grad_up), mm_tn(cot, hidden_low)], 1
        )
        ffn_own = scatter_grads(at, ffn_grads)
        ffn_out = at.permute(at.collect(mm_nt(hidden_low, down_w).reshape(2, 2, rows, width)))
        mixed = (resid + ffn_out).astype(bf16).reshape(tokens.shape)

        grad_resid = grad_ffn.astype(f32) + norm_back(normed_mid, scale_mid, grad_mid)
        grad_attn = grad_resid.astype(bf16)
        grad_mixed = at.permute(mm_nt(grad_attn, out_w).astype(bf16))
        grad_mixed = grad_mixed.reshape(rows, 2, 2, own_heads, size).transpose(1, 2, 3, 0, 4)
        keep = pick(at.pair, grad_mixed[0], grad_mixed[1])
        send = pick(at.pair, grad_mixed[1], grad_mixed[0])
        v = order(at.pair, keep[None], at.pair_swap(send)[None], 0)
        keep, send = pick(at.core, v[:, 0], v[:, 1]), pick(at.core, v[:, 1], v[:, 0])
        v = order(at.core, keep[:, None], at.core_swap(send)[:, None], 1)
        grad_mixed = v.reshape(4, own_heads, rows, size).astype(f32)
        out_grad = mm_tn(own, grad_attn).reshape(width, 2, 2, own_width).transpose(1, 2, 0, 3)
        out_grad = at.collect(out_grad)

        grad_update = (grad_mixed * normed_heads).astype(bf16)
        grad_raw = norm_back(normed_heads, scale_heads, grad_mixed * update).astype(bf16)
        grad_prefix = ein("bhte,bhtf->bhef", query_scaled, grad_raw)
        suffix = [jnp.zeros_like(before)]
        for b in range(4):
            suffix.append(factor * suffix[b] + grad_prefix[3 - b])
        after = jnp.zeros_like(before)
        weight = jnp.ones_like(far)
        for k in range(1, at.groups):
            after = after + weight * at.group_shift(suffix[4], -k)
            weight = weight * far
        grad_weight = ein("bhte,bhse->bhts", grad_raw, values)
        grad_scores = (grad_weight * mask).astype(bf16)
        grad_query = ein("bhts,bhse->bhte", grad_scores, keys)
        grad_key = ein("bhts,bhte->bhse", grad_scores, queries)
        grad_value = ein("bhts,bhte->bhse", weight_low, grad_raw)
        grad_qscaled = ein("bhtf,bhef->bhte", grad_raw, prefix_low)
        full = []
        weight = jnp.ones_like(factor)
        for b in range(4):
            full.append(suffix[b] + weight * after)
            weight = weight * factor
        state_low = jnp.stack(full[::-1]).astype(bf16)
        grad_kscaled = ein("bhsf,bhef->bhse", values, state_low)
        grad_value = (grad_value + ein("bhse,bhef->bhsf", key_scaled, state_low)).astype(bf16)
        grad_qact = grad_query + grad_qscaled * query_decay
        grad_kact = grad_key + grad_kscaled * key_decay
        grad_qpre = (
            rotate(grad_qact, cosine, -sine) * query_sig * (1.0 + query_pre * (1.0 - query_sig))
        ).astype(bf16)
        grad_kpre = (
            rotate(grad_kact, cosine, -sine) * key_sig * (1.0 + key_pre * (1.0 - key_sig))
        ).astype(bf16)
        grads = jnp.stack([grad_qpre, grad_kpre, grad_value, grad_update])
        grads = grads.transpose(1, 3, 0, 2, 4).reshape(4 * rows, 4 * own_width)
        attn_grads = jnp.concatenate([mm_tn(h1, grads), out_grad], 1)
        attn_own = scatter_grads(at, attn_grads)
        grad_in = at.permute(at.collect(mm_nt(grads, attn_w).reshape(2, 2, rows, width)))
        tokens_grad = (grad_resid + norm_back(normed_in, scale_in, grad_in)).reshape(tokens.shape)

        def owned(v, first, count):
            return v[:, :, first : first + count].reshape(v.shape[0], -1)

        return (
            mixed,
            tokens_grad,
            owned(attn_own, 0, own_width),
            owned(attn_own, own_width, own_width),
            owned(attn_own, 2 * own_width, own_width),
            owned(attn_own, 3 * own_width, own_width),
            owned(attn_own, 4 * own_width, own_width),
            owned(ffn_own, 0, hidden),
            owned(ffn_own, wide, hidden),
            owned(ffn_own, 2 * wide, hidden).T,
        )

    return body


def solution(mesh):
    act = P("items", "seq", None)
    row = P(("items", "seq"), None)
    col = P(None, ("items", "seq"))
    return jax.shard_map(
        make_body(mesh.shape["items"], mesh.shape["seq"]),
        mesh=mesh,
        in_specs=(act, P()) + (row,) * 7 + (col, act),
        out_specs=(act, act) + (row,) * 7 + (col,),
        check_vma=False,
    )
```

```python
import functools
import math

import jax
import jax.numpy as jnp
from jax import lax
from jax.experimental import pallas as pl
from jax.experimental.pallas import tpu as pltpu
from jax.sharding import PartitionSpec as P

epsilon = 1e-06
AXES = ("items", "seq")
f32 = jnp.float32
bf16 = jnp.bfloat16
MIB = 1024 * 1024


def mm(a, b):
    return jnp.dot(a, b, preferred_element_type=f32)


def mm_tn(a, b):
    return lax.dot_general(a, b, (((0,), (0,)), ((), ())), preferred_element_type=f32)


def mm_nt(a, b):
    return lax.dot_general(a, b, (((1,), (1,)), ((), ())), preferred_element_type=f32)


def norm_factor(v):
    return lax.rsqrt(jnp.mean(v * v, axis=-1, keepdims=True) + epsilon)


def norm_back(normed, scale, grad):
    return scale * (grad - normed * jnp.mean(grad * normed, axis=-1, keepdims=True))


def like(shape, dtype):
    return jax.ShapeDtypeStruct(tuple(shape), dtype)


def run(name, kernel, outs, scalars, arrays, scratch=(), flops=0, vmem=24):
    ins = list(scalars) + list(arrays)
    size = sum(v.size * v.dtype.itemsize for v in list(arrays) + list(outs))
    return pl.pallas_call(
        kernel,
        out_shape=list(outs),
        in_specs=[pl.BlockSpec(memory_space=pltpu.SMEM)] * len(scalars)
        + [pl.BlockSpec(memory_space=pltpu.VMEM)] * len(arrays),
        out_specs=[pl.BlockSpec(memory_space=pltpu.VMEM)] * len(outs),
        scratch_shapes=list(scratch),
        compiler_params=pltpu.CompilerParams(vmem_limit_bytes=vmem * MIB),
        cost_estimate=pl.CostEstimate(flops=flops, bytes_accessed=size, transcendentals=0),
        name=name,
    )(*ins)


class Place:
    def __init__(self, items, seqs):
        self.items, self.seqs, self.groups = items, seqs, seqs // 4
        self.count = items * seqs
        self.item = lax.axis_index("items")
        where = lax.axis_index("seq")
        self.group, self.member = where // 4, where % 4

    def swap(self, v, mask):
        return lax.ppermute(v, AXES, [(d, d ^ mask) for d in range(self.count)])

    def group_swap(self, v, k):
        return self.swap(v, 4 * k)

    def item_swap(self, v, k):
        return self.swap(v, self.seqs * k)

    def group_shift(self, v, k):
        pairs = []
        for d in range(self.count):
            g = (d % self.seqs) // 4 + k
            if 0 <= g < self.groups:
                pairs.append((d, d + 4 * k))
        return lax.ppermute(v, AXES, pairs)

    def spread(self, v):
        far = self.swap(v, 2)
        return [v, self.swap(v, 1), far, self.swap(far, 1)]

    def exchange(self, parts):
        return [parts[0]] + [self.swap(parts[d], d) for d in (1, 2, 3)]

    def collect(self, keep0, send1, keep2, send3):
        got3 = self.swap(send3, 1)
        far = self.swap((keep2 + got3.astype(f32)).astype(bf16), 2)
        got1 = self.swap(send1, 1)
        return [keep0, got1, far]

    def in_order(self, parts):
        out = None
        for m in (3, 2, 1, 0):
            v = jnp.concatenate([parts[m ^ k] for k in range(4)], 0)
            out = v if out is None else jnp.where(self.member == m, v, out)
        return out


def blocks_of(ref, count, size, first):
    if count == 1:
        return ref[...]
    return jnp.concatenate(
        [ref[:, pl.ds(pl.multiple_of((k ^ first) * size, size), size)] for k in range(count)], 1
    )


def rows_of(refs):
    if len(refs) == 1:
        return refs[0][...]
    return jnp.concatenate([r[...] for r in refs], 0)


def pack_attn_kernel(own, width, info, q, k, v, u, *outs):
    member = info[0]
    for d in range(4):
        for n, ref in enumerate((q, k, v, u)):
            place = pl.ds(pl.multiple_of((member ^ d) * own, own), own)
            outs[d][:, n * own : (n + 1) * own] = ref[:, place]


def pack_ffn_kernel(own, hidden, wide, info, g, u, dn, o, *outs):
    member = info[0]
    for m in range(4):

        @pl.when(member == m)
        def _():
            for d in range(4):
                j = m ^ d
                for n, ref in enumerate((g, u, dn)):
                    v = ref[:, j * hidden : (j + 1) * hidden]
                    if wide != hidden:
                        v = jnp.concatenate(
                            [v, jnp.zeros((v.shape[0], wide - hidden), v.dtype)], 1
                        )
                    outs[d][:, n * wide : (n + 1) * wide] = v
                outs[d][:, 3 * wide :] = o[:, j * own : (j + 1) * own]


def prep_kernel(count, block, info, x, c, h_out, c_out, scr):
    first = info[1]
    v = x[...].astype(f32)
    scr[...] = v * norm_factor(v)
    h_out[...] = blocks_of(scr, count, block, first).astype(bf16)
    scr[...] = c[...].astype(f32)
    c_out[...] = blocks_of(scr, count, block, first).astype(bf16)


def turn(v, cosine, sine):
    return v * cosine + pltpu.roll(v, v.shape[-1] // 2, 1) * sine


def project_kernel(nw, own, size, info, fac, *refs):
    h, w = refs[:4], refs[4 : 4 + nw]
    cosine, sine, qd, kd = refs[4 + nw : 8 + nw]
    q0, k0, u, v, q, k, qs, ks, prefix, total, local = refs[8 + nw :]
    member = info[0]
    heads = own // size
    for d in range(4):
        weights = rows_of(w)
        pre = mm(h[d][...], weights)
        q0[d] = pre[:, :own]
        k0[d] = pre[:, own : 2 * own]
        v[d] = pre[:, 2 * own : 3 * own].astype(bf16)
        u[d] = pre[:, 3 * own :]
        for n in range(heads):
            lanes = slice(n * size, (n + 1) * size)
            z = q0[d, :, lanes]
            act = turn(z * jax.nn.sigmoid(z), cosine[d], sine[d])
            q[d, :, lanes] = act.astype(bf16)
            qs[d, :, lanes] = (act * qd[n]).astype(bf16)
            z = k0[d, :, lanes]
            act = turn(z * jax.nn.sigmoid(z), cosine[d], sine[d])
            k[d, :, lanes] = act.astype(bf16)
            scaled = (act * kd[n]).astype(bf16)
            ks[d, :, lanes] = scaled
            local[member ^ d, n] = mm_tn(scaled, v[d, :, lanes])
    for n in range(heads):
        state = jnp.zeros((size, size), f32)
        for b in range(4):
            prefix[b, n] = state
            state = fac[n, 1] * state + local[b, n]
        total[n] = state


def scores_kernel(own, size, q, k, v, mask, w, intra):
    for d in range(4):
        for n in range(own // size):
            lanes = slice(n * size, (n + 1) * size)
            low = (mm_nt(q[d, :, lanes], k[d, :, lanes]) * mask[n]).astype(bf16)
            w[d, n] = low
            intra[d, :, lanes] = mm(low, v[d, :, lanes])


def attend_kernel(own, size, info, fac, prefix, before, qs, intra, u, plow, attn, *z):
    member = info[0]
    for d in range(4):
        b = member ^ d
        for n in range(own // size):
            lanes = slice(n * size, (n + 1) * size)
            low = (prefix[b, n] + fac[n, b] * before[n]).astype(bf16)
            plow[d, n] = low
            a = intra[d, :, lanes] + mm(qs[d, :, lanes], low)
            attn[d, :, lanes] = a
            z[d][:, lanes] = (a * norm_factor(a) * u[d, :, lanes]).astype(bf16)


def mid_kernel(count, block, own, info, x, *refs):
    z, o = refs[:4], refs[4:8]
    y, h2, zp, full, scr = refs[8:]
    member, first = info[0], info[1]
    for d in range(4):
        full[:, pl.ds(pl.multiple_of((member ^ d) * own, own), own)] = z[d][...]
    zp[...] = blocks_of(full, count, block, first)
    mixed = zp[...]
    for d in range(4):
        scr[:, pl.ds(pl.multiple_of((member ^ d) * own, own), own)] = mm(mixed, o[d][...])
    v = x[...].astype(f32) + scr[...]
    y[...] = v
    scr[...] = v * norm_factor(v)
    h2[...] = blocks_of(scr, count, block, first).astype(bf16)


def ffn_kernel(nw, wide, *refs):
    h, c, w = refs[:2], refs[2:4], refs[4 : 4 + nw]
    outs = refs[4 + nw :]
    for d in range(2):
        hd, dg, df, part = outs[4 * d : 4 * d + 4]
        gate = jnp.concatenate([r[:, :wide] for r in w], 0) if nw > 1 else w[0][:, :wide]
        up = jnp.concatenate([r[:, wide : 2 * wide] for r in w], 0) if nw > 1 else w[0][:, wide : 2 * wide]
        down = (
            jnp.concatenate([r[:, 2 * wide : 3 * wide] for r in w], 0)
            if nw > 1
            else w[0][:, 2 * wide : 3 * wide]
        )
        g = mm(h[d][...], gate)
        f = mm(h[d][...], up)
        hd[...] = (g * f).astype(bf16)
        t = mm(c[d][...], down)
        dg[...] = (t * f).astype(bf16)
        df[...] = (t * g).astype(bf16)
        part[...] = (mm_nt(dg[...], gate) + mm_nt(df[...], up)).astype(part.dtype)


def ffn_out_kernel(nw, wide, *refs):
    hd, w, outs = refs[:4], refs[4 : 4 + nw], refs[4 + nw :]
    for d in range(4):
        down = jnp.concatenate([r[:, 2 * wide : 3 * wide] for r in w], 0) if nw > 1 else w[0][:, 2 * wide : 3 * wide]
        outs[d][...] = mm_nt(hd[d][...], down).astype(outs[d].dtype)


def store_grads(outs, items, groups, rows, lanes, value):
    half = groups // 2
    for part, one, two in ((0, 1, 2), (1, 2, 1)):
        send, keep2, keep0 = outs[3 * part : 3 * part + 3]
        for i in range(items):
            lo = (i * groups + part * half) * rows
            v = value[lo : lo + half * rows].astype(bf16)
            if i == 0:
                keep0[:, lanes] = v
            elif i == two:
                keep2[:, lanes] = v
            else:
                send[0 if i == one else 1, :, lanes] = v


def ffn_grad_kernel(items, groups, rows, wide, *refs):
    h, c, dg, df, hd = (refs[4 * n : 4 * n + 4] for n in range(5))
    outs = refs[20:]
    left = jnp.concatenate([r[...] for r in h], 0)
    for n, right in enumerate((dg, df)):
        value = mm_tn(left, jnp.concatenate([r[...] for r in right], 0))
        store_grads(outs, items, groups, rows, slice(n * wide, (n + 1) * wide), value)
    left = jnp.concatenate([r[...] for r in c], 0)
    value = mm_tn(left, jnp.concatenate([r[...] for r in hd], 0))
    store_grads(outs, items, groups, rows, slice(2 * wide, 3 * wide), value)


def mid_back_kernel(count, block, own, info, y, cot, a0, a1, a2, *refs):
    o = refs[:4]
    dy, do, z0, z1, z2, z3, scr = refs[4:]
    z = (z0, z1, z2, z3)
    member, first = info[0], info[1]
    scr[...] = a0[...] + a1[...].astype(f32) + a2[...].astype(f32)
    grad = blocks_of(scr, count, block, first)
    v = y[...]
    scale = norm_factor(v)
    v = cot[...].astype(f32) + norm_back(v * scale, scale, grad)
    dy[...] = v
    do[...] = v.astype(bf16)
    total = None
    for d in range(4):
        part = do[:, pl.ds(pl.multiple_of((member ^ d) * own, own), own)]
        t = mm_nt(part, o[d][...])
        total = t if total is None else total + t
    scr[...] = total
    scr[...] = blocks_of(scr, count, block, first)
    for d in range(4):
        z[d][...] = scr[:, pl.ds(pl.multiple_of((member ^ d) * own, own), own)].astype(bf16)


def out_grad_kernel(own, info, zp, do, *outs):
    member = info[0]
    left = zp[...].T
    for d in range(4):
        part = do[:, pl.ds(pl.multiple_of((member ^ d) * own, own), own)]
        outs[d][...] = mm(left, part).astype(outs[d].dtype)


def back_state_kernel(own, size, info, fac, z0, z1, z2, z3, attn, u, qs, du, da, suffix, total, local):
    member = info[0]
    z = (z0, z1, z2, z3)
    heads = own // size
    for d in range(4):
        for n in range(heads):
            lanes = slice(n * size, (n + 1) * size)
            dz = z[d][:, lanes].astype(f32)
            a = attn[d, :, lanes]
            scale = norm_factor(a)
            normed = a * scale
            du[d, :, lanes] = (dz * normed).astype(bf16)
            low = norm_back(normed, scale, dz * u[d, :, lanes]).astype(bf16)
            da[d, :, lanes] = low
            local[member ^ d, n] = mm_tn(qs[d, :, lanes], low)
    for n in range(heads):
        state = jnp.zeros((size, size), f32)
        for b in (3, 2, 1, 0):
            suffix[b, n] = state
            state = fac[n, 1] * state + local[b, n]
        total[n] = state


def back_local_kernel(own, size, da, v, w, q, k, plow, mask, qd, dq, dk, dv):
    for d in range(4):
        for n in range(own // size):
            lanes = slice(n * size, (n + 1) * size)
            a = da[d, :, lanes]
            ds = (mm_nt(a, v[d, :, lanes]) * mask[n]).astype(bf16)
            dq[d, :, lanes] = mm(ds, k[d, :, lanes]) + mm_nt(a, plow[d, n]) * qd[n]
            dk[d, :, lanes] = mm_tn(ds, q[d, :, lanes])
            dv[d, :, lanes] = mm_tn(w[d, n], a)


def back_final_kernel(nw, own, size, info, fac, suffix, after, v, ks, du, dq, dk, dv, q0, k0, cosine, sine, kd, *refs):
    w, outs = refs[:nw], refs[nw:]
    grads = outs[0]
    parts = outs[1:]
    member = info[0]
    for d in range(4):
        b = member ^ d
        for n in range(own // size):
            lanes = slice(n * size, (n + 1) * size)
            low = (suffix[b, n] + fac[n, 3 - b] * after[n]).astype(bf16)
            dka = dk[d, :, lanes] + mm_nt(v[d, :, lanes], low) * kd[n]
            dvv = dv[d, :, lanes] + mm(ks[d, :, lanes], low)
            z = q0[d, :, lanes]
            s = jax.nn.sigmoid(z)
            g = turn(dq[d, :, lanes], cosine[d], -sine[d]) * s * (1.0 + z * (1.0 - s))
            grads[d, :, n * size : (n + 1) * size] = g.astype(bf16)
            z = k0[d, :, lanes]
            s = jax.nn.sigmoid(z)
            g = turn(dka, cosine[d], -sine[d]) * s * (1.0 + z * (1.0 - s))
            grads[d, :, own + n * size : own + (n + 1) * size] = g.astype(bf16)
            grads[d, :, 2 * own + n * size : 2 * own + (n + 1) * size] = dvv.astype(bf16)
        grads[d, :, 3 * own :] = du[d]
        parts[d][...] = mm_nt(grads[d], rows_of(w)).astype(parts[d].dtype)


def attn_grad_kernel(items, groups, rows, wide, h0, h1, h2, h3, grads, *outs):
    left = jnp.concatenate([h0[...], h1[...], h2[...], h3[...]], 0)
    value = mm_tn(left, jnp.concatenate([grads[d] for d in range(4)], 0))
    store_grads(outs, items, groups, rows, slice(0, wide), value)


def first_back_kernel(count, block, info, x, dy, a0, a1, a2, out, scr):
    scr[...] = a0[...] + a1[...].astype(f32) + a2[...].astype(f32)
    grad = blocks_of(scr, count, block, info[1])
    v = x[...].astype(f32)
    scale = norm_factor(v)
    out[...] = dy[...] + norm_back(v * scale, scale, grad)


def mixed_kernel(count, block, info, y, a0, a1, a2, out, scr):
    scr[...] = a0[...] + a1[...].astype(f32) + a2[...].astype(f32)
    out[...] = (y[...] + blocks_of(scr, count, block, info[1])).astype(bf16)


def final_kernel(widths, own_cols, info, p0, p1, p2, p3, *outs):
    member = info[0]
    parts = (p0, p1, p2, p3)
    for m in range(4):

        @pl.when(member == m)
        def _():
            for d in range(4):
                j = m ^ d
                lo = 0
                for out, wide, cols in zip(outs, widths, own_cols):
                    out[:, j * cols : (j + 1) * cols] = parts[d][:, lo : lo + cols].astype(f32)
                    lo += wide


def gather_rows(at, v):
    pieces = [v] + [at.group_swap(v, k) for k in range(1, at.groups)]
    half = at.groups // 2
    table = {}
    for k, piece in enumerate(pieces):
        one, two = (1, 2) if k < half else (2, 1)
        first = at.item_swap(piece, one)
        second = at.item_swap(piece, two)
        table[0, k], table[one, k], table[two, k] = piece, first, second
        table[3, k] = at.item_swap(first, two)
    return [table[i, k] for i in range(at.items) for k in range(at.groups)]


def scatter_rows(at, outs, rows, wide):
    half = at.groups // 2
    sums = []
    for part, one, two in ((0, 1, 2), (1, 2, 1)):
        send, keep2, keep0 = outs[3 * part : 3 * part + 3]
        got = at.item_swap(send, one)
        far = at.item_swap((keep2.astype(f32) + got[1].astype(f32)).astype(bf16), two)
        sums.append((keep0, got, far))

    def total_of(part, k):
        keep0, got, far = sums[part]
        rows_k = slice(k * rows, (k + 1) * rows)
        return keep0[rows_k].astype(f32) + got[0, rows_k].astype(f32) + far[rows_k].astype(f32)

    away = [
        at.group_swap(total_of(k // half, k % half).astype(bf16), k) for k in range(1, at.groups)
    ]
    total = total_of(0, 0)
    for v in away:
        total = total + v.astype(f32)
    return total


def by_rows(at, total):
    rows = total.shape[0] // 4
    parts = [
        lax.dynamic_slice_in_dim(total, (at.member ^ d) * rows, rows, 0) for d in range(4)
    ]
    return at.exchange([parts[0]] + [v.astype(bf16) for v in parts[1:]])


def rotation_tables(positions, head_size):
    half_width = head_size // 2
    pair_index = jnp.arange(half_width, dtype=jnp.int32)
    step_sizes = jnp.right_shift(jnp.full((half_width,), 8192, jnp.int32), pair_index // 5)
    phase_int = positions[:, None] * step_sizes[None, :] % 65536
    angles = phase_int.astype(f32) * (2.0 * math.pi / 65536.0)
    return (jnp.cos(angles), jnp.sin(angles))


def make_body(items, seqs):
    def body(
        tokens,
        decay_rate,
        query_weight,
        key_weight,
        value_weight,
        update_weight,
        output_weight,
        gate_weight,
        up_weight,
        down_weight,
        cotangent,
    ):
        at = Place(items, seqs)
        groups = at.groups
        width = tokens.shape[-1]
        rows = tokens.shape[1]
        heads = decay_rate.shape[0]
        size = width // heads
        own_heads = heads // 4
        own = width // 4
        shard = query_weight.shape[0]
        hidden = gate_weight.shape[1] // 4
        wide = hidden + -hidden % 256
        count, block = items * groups, 4 * shard
        first = at.item * groups + at.group
        aligned = block % 128 == 0
        if aligned:
            info = jnp.stack([at.member, first])
            kcount, kblock = count, block
        else:
            info = jnp.stack([at.member, jnp.zeros_like(first)])
            kcount, kblock = 1, width
        info = info.astype(jnp.int32)

        def arrange(pieces):
            if aligned:
                return pieces
            v = jnp.stack(pieces)
            return [v[jnp.arange(count) ^ first].reshape(width, -1)]

        def act(dtype=bf16):
            return like((rows, width), dtype)

        blk = functools.partial(like, (4, rows, own))
        x = tokens.reshape(rows, width)
        cot = cotangent.reshape(rows, width)

        aw = run(
            "pack_attn",
            functools.partial(pack_attn_kernel, own, width),
            [like((shard, 4 * own), bf16)] * 4,
            [info],
            [query_weight, key_weight, value_weight, update_weight],
        )
        fw = run(
            "pack_ffn",
            functools.partial(pack_ffn_kernel, own, hidden, wide),
            [like((shard, 3 * wide + own), bf16)] * 4,
            [info],
            [gate_weight, up_weight, down_weight.T, output_weight],
        )
        attn_w = arrange(gather_rows(at, at.in_order(at.exchange(aw))))
        h1_own, cot_own = run(
            "prep",
            functools.partial(prep_kernel, kcount, kblock),
            [act(), act()],
            [info],
            [x, cot],
            [pltpu.VMEM((rows, width), f32)],
        )
        h1 = at.spread(h1_own)
        ffn_w = arrange(gather_rows(at, at.in_order(at.exchange(fw))))
        out_w = at.spread(jnp.concatenate([v[:, 3 * wide :] for v in ffn_w], 0))
        cots = at.spread(cot_own)
        nw = len(attn_w)

        blocks = at.group * 4 + (at.member ^ jnp.arange(4, dtype=jnp.int32))
        positions = (blocks[:, None] * rows + jnp.arange(rows, dtype=jnp.int32)).reshape(-1)
        cosine, sine = rotation_tables(positions, size)
        cosine = jnp.concatenate([cosine, cosine], 1).reshape(4, rows, size)
        sine = jnp.concatenate([-sine, sine], 1).reshape(4, rows, size)
        log_decay = lax.dynamic_slice(jnp.log(decay_rate), (at.member * own_heads,), (own_heads,))
        local = jnp.arange(rows).astype(f32)
        ld = log_decay[:, None]
        query_decay = jnp.broadcast_to(
            jnp.exp(ld * (local + 1.0))[:, :, None], (own_heads, rows, size)
        )
        key_decay = jnp.broadcast_to(
            jnp.exp(ld * (rows - 1.0 - local))[:, :, None], (own_heads, rows, size)
        )
        offset = local[:, None] - local[None, :]
        mask = jnp.where(
            offset >= 0.0, jnp.exp(log_decay[:, None, None] * jnp.maximum(offset, 0.0)), 0.0
        )
        fac = jnp.exp(ld * rows * jnp.arange(4).astype(f32))
        group_fac = jnp.exp(log_decay * (4.0 * rows))[:, None, None]

        state = like((own_heads, size, size), f32)
        states = like((4, own_heads, size, size), f32)
        states_low = like((4, own_heads, size, size), bf16)
        scratch_states = pltpu.VMEM((4, own_heads, size, size), f32)

        def carried(total, sign):
            out = at.group_shift(total, sign)
            weight = group_fac
            for k in range(2, groups):
                out = out + weight * at.group_shift(total, sign * k)
                weight = weight * group_fac
            return out

        q0, k0, u, v, q, k, qs, ks, prefix, total = run(
            "project",
            functools.partial(project_kernel, nw, own, size),
            [blk(f32), blk(f32), blk(f32)] + [blk(bf16)] * 5 + [states, state],
            [info, fac],
            h1 + attn_w + [cosine, sine, query_decay, key_decay],
            [scratch_states],
            flops=8 * rows * width * 4 * own,
            vmem=32,
        )
        before = carried(total, 1)
        w, intra = run(
            "scores",
            functools.partial(scores_kernel, own, size),
            [like((4, own_heads, rows, rows), bf16), blk(f32)],
            [],
            [q, k, v, mask],
            flops=16 * rows * rows * own,
        )
        plow, attn, *z = run(
            "attend",
            functools.partial(attend_kernel, own, size),
            [states_low, blk(f32)] + [like((rows, own), bf16)] * 4,
            [info, fac],
            [prefix, before, qs, intra, u],
            flops=8 * rows * size * own,
        )
        z = at.exchange(z)
        y, h2_own, zp = run(
            "mid",
            functools.partial(mid_kernel, kcount, kblock, own),
            [act(f32), act(), act()],
            [info],
            [x] + z + out_w,
            [pltpu.VMEM((rows, width), bf16), pltpu.VMEM((rows, width), f32)],
            flops=2 * rows * width * width,
        )
        h2 = at.spread(h2_own)

        hid = like((rows, wide), bf16)
        ffn = [None] * 4
        for pair in ((2, 3), (0, 1)):
            res = run(
                "ffn%d" % pair[0],
                functools.partial(ffn_kernel, nw, wide),
                [hid] * 3 + [act(f32)] + [hid] * 3 + [act()],
                [],
                [h2[d] for d in pair] + [cots[d] for d in pair] + ffn_w,
                flops=20 * rows * width * wide,
                vmem=40,
            )
            ffn[pair[0]], ffn[pair[1]] = res[:4], res[4:]
        hd, dg, df, part = (list(t) for t in zip(*ffn))
        mid_sums = at.collect(*part)

        def grad_outs(cols):
            half = groups // 2 * block
            return [
                like((2, half, cols), bf16),
                like((half, cols), bf16),
                like((half, cols), bf16),
            ] * 2

        ffn_outs = run(
            "ffn_grad",
            functools.partial(ffn_grad_kernel, items, groups, block, wide),
            grad_outs(3 * wide),
            [],
            h2 + cots + dg + df + hd,
            flops=24 * rows * width * wide,
            vmem=48,
        ) if aligned else None
        ffn_parts = run(
            "ffn_out",
            functools.partial(ffn_out_kernel, nw, wide),
            [act(f32), act(), act(f32), act()],
            [],
            hd + ffn_w,
            flops=8 * rows * width * wide,
            vmem=32,
        )

        def split_grads(g):
            g = g.astype(bf16).reshape(count, block, -1)[jnp.arange(count) ^ first]
            g = g.reshape(items, groups // 2 * 2, block, -1)
            half = groups // 2
            res = []
            for p, one, two in ((0, 1, 2), (1, 2, 1)):
                t = g[:, p * half : (p + 1) * half].reshape(items, half * block, -1)
                res += [jnp.stack([t[one], t[3]]), t[two], t[0]]
            return res

        if not aligned:
            hh, cc = jnp.concatenate(h2, 0), jnp.concatenate(cots, 0)
            ffn_outs = split_grads(
                jnp.concatenate(
                    [
                        mm_tn(hh, jnp.concatenate(dg, 0)),
                        mm_tn(hh, jnp.concatenate(df, 0)),
                        mm_tn(cc, jnp.concatenate(hd, 0)),
                    ],
                    1,
                )
            )
        ffn_own = by_rows(at, scatter_rows(at, ffn_outs, block, 3 * wide))
        mixed = run(
            "mixed",
            functools.partial(mixed_kernel, kcount, kblock),
            [act()],
            [info],
            [y] + at.collect(*ffn_parts),
            [pltpu.VMEM((rows, width), f32)],
        )[0]

        dy, do, *dz = run(
            "mid_back",
            functools.partial(mid_back_kernel, kcount, kblock, own),
            [act(f32), act()] + [like((rows, own), bf16)] * 4,
            [info],
            [y, cot] + mid_sums + out_w,
            [pltpu.VMEM((rows, width), f32)],
            flops=2 * rows * width * width,
        )
        dz = at.exchange(dz)
        og = run(
            "out_grad",
            functools.partial(out_grad_kernel, own),
            [like((width, own), f32), like((width, own), bf16)] * 2,
            [info],
            [zp, do],
            flops=2 * rows * width * width,
        )
        og = at.collect(*og)
        og = og[0] + og[1].astype(f32) + og[2].astype(f32)

        du, da, suffix, gtotal = run(
            "back_state",
            functools.partial(back_state_kernel, own, size),
            [blk(bf16), blk(bf16), states, state],
            [info, fac],
            dz + [attn, u, qs],
            [scratch_states],
            flops=8 * rows * size * own,
        )
        after = carried(gtotal, -1)
        dq, dk, dv = run(
            "back_local",
            functools.partial(back_local_kernel, own, size),
            [blk(f32)] * 3,
            [],
            [da, v, w, q, k, plow, mask, query_decay],
            flops=40 * rows * rows * own,
        )
        grads, *part = run(
            "back_final",
            functools.partial(back_final_kernel, nw, own, size),
            [like((4, rows, 4 * own), bf16), act(f32), act(), act(f32), act()],
            [info, fac],
            [suffix, after, v, ks, du, dq, dk, dv, q0, k0, cosine, sine, key_decay] + attn_w,
            flops=8 * rows * width * 4 * own,
            vmem=40,
        )
        if aligned:
            attn_outs = run(
                "attn_grad",
                functools.partial(attn_grad_kernel, items, groups, block, 4 * own),
                grad_outs(4 * own),
                [],
                h1 + [grads],
                flops=8 * rows * width * 4 * own,
                vmem=40,
            )
            og_half = groups // 2 * block
            og4 = og.astype(bf16).reshape(items, 2, og_half, own)
        else:
            attn_outs = split_grads(
                mm_tn(jnp.concatenate(h1, 0), grads.reshape(4 * rows, 4 * own))
            )
        if aligned:
            og_outs = []
            for p, one, two in ((0, 1, 2), (1, 2, 1)):
                og_outs += [jnp.stack([og4[one, p], og4[3, p]]), og4[two, p], og4[0, p]]
        else:
            og_outs = split_grads(og)
        attn_own = by_rows(at, scatter_rows(at, attn_outs, block, 4 * own))
        out_own = by_rows(at, scatter_rows(at, og_outs, block, own))
        tokens_grad = run(
            "first_back",
            functools.partial(first_back_kernel, kcount, kblock),
            [act(f32)],
            [info],
            [x, dy] + at.collect(*part),
            [pltpu.VMEM((rows, width), f32)],
        )[0]
        qg, kg, vg, ug = run(
            "final_attn",
            functools.partial(final_kernel, (own,) * 4, (own,) * 4),
            [like((shard, width), f32)] * 4,
            [info],
            attn_own,
        )
        (wg,) = run(
            "final_out",
            functools.partial(final_kernel, (own,), (own,)),
            [like((shard, width), f32)],
            [info],
            out_own,
        )
        gg, pg, ng = run(
            "final_ffn",
            functools.partial(final_kernel, (wide,) * 3, (hidden,) * 3),
            [like((shard, 4 * hidden), f32)] * 3,
            [info],
            ffn_own,
        )
        return (
            mixed.reshape(tokens.shape),
            tokens_grad.reshape(tokens.shape),
            qg,
            kg,
            vg,
            ug,
            wg,
            gg,
            pg,
            ng.T,
        )

    return body


def solution(mesh):
    act = P("items", "seq", None)
    row = P(("items", "seq"), None)
    col = P(None, ("items", "seq"))
    return jax.shard_map(
        make_body(mesh.shape["items"], mesh.shape["seq"]),
        mesh=mesh,
        in_specs=(act, P()) + (row,) * 7 + (col, act),
        out_specs=(act, act) + (row,) * 7 + (col,),
        check_vma=False,
    )
```

```python
import functools
import math

import jax
import jax.numpy as jnp
from jax import lax
from jax.experimental import pallas as pl
from jax.experimental.pallas import tpu as pltpu
from jax.sharding import PartitionSpec as P

epsilon = 1e-06
AXES = ("items", "group", "member")
f32 = jnp.float32
bf16 = jnp.bfloat16
MIB = 1024 * 1024
VM = (12, 16, 16, 16)


def mm(a, b):
    return jnp.dot(a, b, preferred_element_type=f32)


def mm_tn(a, b):
    return lax.dot_general(a, b, (((0,), (0,)), ((), ())), preferred_element_type=f32)


def mm_nt(a, b):
    return lax.dot_general(a, b, (((1,), (1,)), ((), ())), preferred_element_type=f32)


def norm_factor(v):
    return lax.rsqrt(jnp.mean(v * v, axis=-1, keepdims=True) + epsilon)


def norm_back(normed, scale, grad):
    return scale * (grad - normed * jnp.mean(grad * normed, axis=-1, keepdims=True))


def like(shape, dtype):
    return jax.ShapeDtypeStruct(tuple(shape), dtype)


def run(name, kernel, outs, scalars, arrays, scratch=(), flops=0, vmem=10, after=()):
    ins = list(scalars) + list(arrays) + list(after)
    used, held = len(scalars) + len(arrays), len(after)

    def body(*refs):
        kernel(*refs[:used], *refs[used + held :])

    size = sum(v.size * v.dtype.itemsize for v in list(arrays) + list(outs)) if flops else 0
    return pl.pallas_call(
        body,
        out_shape=list(outs),
        in_specs=[pl.BlockSpec(memory_space=pltpu.SMEM)] * len(scalars)
        + [pl.BlockSpec(memory_space=pltpu.VMEM)] * len(arrays)
        + [pl.BlockSpec(memory_space=pl.ANY)] * held,
        out_specs=[pl.BlockSpec(memory_space=pltpu.VMEM)] * len(outs),
        scratch_shapes=list(scratch),
        compiler_params=pltpu.CompilerParams(vmem_limit_bytes=vmem * MIB),
        cost_estimate=pl.CostEstimate(flops=flops, bytes_accessed=size, transcendentals=0),
        name=name,
    )(*ins)


def tie(v, *after):
    anywhere = pl.BlockSpec(memory_space=pl.ANY)
    return pl.pallas_call(
        lambda *refs: None,
        out_shape=like(v.shape, v.dtype),
        in_specs=[anywhere] * (1 + len(after)),
        out_specs=anywhere,
        input_output_aliases={0: 0},
        compiler_params=pltpu.CompilerParams(vmem_limit_bytes=MIB),
        name="tie",
        cost_estimate=pl.CostEstimate(flops=0, bytes_accessed=0, transcendentals=0),
    )(v, *after)


class Place:
    def __init__(self, items, seqs):
        self.items, self.seqs, self.groups = items, seqs, seqs // 4
        self.count = items * seqs
        self.item, self.group, self.member = (lax.axis_index(name) for name in AXES)

    def swap(self, v, mask):
        return lax.ppermute(v, AXES, [(d, d ^ mask) for d in range(self.count)])

    def group_swap(self, v, k):
        return self.swap(v, 4 * k)

    def item_swap(self, v, k):
        return self.swap(v, self.seqs * k)

    def group_shift(self, v, k):
        pairs = []
        for d in range(self.count):
            g = (d % self.seqs) // 4 + k
            if 0 <= g < self.groups:
                pairs.append((d, d + 4 * k))
        return lax.ppermute(v, AXES, pairs)

    def spread(self, v):
        far = self.swap(v, 2)
        return [v, self.swap(v, 1), far, self.swap(far, 1)]

    def exchange(self, parts):
        return [parts[0]] + [self.swap(parts[d], d) for d in (1, 2, 3)]

    def collect_far(self, keep2, send3, after=()):
        pair = [keep2, self.swap(send3, 1)]
        (v,) = run("add", add_kernel, [like(keep2.shape, bf16)], [], pair, after=after)
        return v, self.swap(v, 2)

    def collect(self, keep0, send1, keep2, send3, after=()):
        far = self.collect_far(keep2, send3, after)[1]
        return [keep0, self.swap(send1, 1), far]

    def in_order(self, parts):
        out = None
        for m in (3, 2, 1, 0):
            v = jnp.concatenate([parts[m ^ k] for k in range(4)], 0)
            out = v if out is None else jnp.where(self.member == m, v, out)
        return out


def blocks_of(ref, count, size, first):
    if count == 1:
        return ref[...]
    return jnp.concatenate(
        [ref[:, pl.ds(pl.multiple_of((k ^ first) * size, size), size)] for k in range(count)], 1
    )


def rows_of(refs):
    if len(refs) == 1:
        return refs[0][...]
    return jnp.concatenate([r[...] for r in refs], 0)


def pack_kernel(own, hidden, wide, info, q, k, v, u, o, g, up, dn, *refs):
    outs, small, large, sems = refs[:4], refs[4], refs[5], refs[6]
    copies = [
        pltpu.make_async_copy(ref, small.at[n], sems.at[n]) for n, ref in enumerate((q, k, v, u, o))
    ] + [pltpu.make_async_copy(ref, large.at[n], sems.at[5 + n]) for n, ref in enumerate((g, up, dn))]
    for copy in copies:
        copy.start()
    for copy in copies:
        copy.wait()
    member = info[0]
    for m in range(4):

        @pl.when(member == m)
        def _():
            for d in range(4):
                j = m ^ d
                for n in range(5):
                    outs[d][:, n * own : (n + 1) * own] = small[n, :, j * own : (j + 1) * own]
                for n in range(3):
                    v = large[n, :, j * hidden : (j + 1) * hidden]
                    if wide != hidden:
                        v = jnp.concatenate(
                            [v, jnp.zeros((v.shape[0], wide - hidden), v.dtype)], 1
                        )
                    lo = 5 * own + n * wide
                    outs[d][:, lo : lo + wide] = v


def prep_kernel(count, block, info, x, c, h_out, c_out, scr):
    first = info[1]
    v = x[...].astype(f32)
    scr[...] = v * norm_factor(v)
    h_out[...] = blocks_of(scr, count, block, first).astype(bf16)
    scr[...] = c[...].astype(f32)
    c_out[...] = blocks_of(scr, count, block, first).astype(bf16)


def turn(v, cosine, sine):
    return v * cosine + pltpu.roll(v, v.shape[-1] // 2, 1) * sine


def project_kernel(nw, own, size, info, fac, *refs):
    h, w = refs[:4], refs[4 : 4 + nw]
    cosine, sine, qd, kd = refs[4 + nw : 8 + nw]
    q0, k0, u, v, q, k, qs, ks, prefix, total, out_w, local = refs[8 + nw :]
    member = info[0]
    out_w[...] = jnp.concatenate([r[:, 4 * own :] for r in w], 0)
    heads = own // size
    for d in range(4):
        weights = jnp.concatenate([r[:, : 4 * own] for r in w], 0)
        pre = mm(h[d][...], weights)
        q0[d] = pre[:, :own]
        k0[d] = pre[:, own : 2 * own]
        v[d] = pre[:, 2 * own : 3 * own].astype(bf16)
        u[d] = pre[:, 3 * own :]
        for n in range(heads):
            lanes = slice(n * size, (n + 1) * size)
            z = q0[d, :, lanes]
            act = turn(z * jax.nn.sigmoid(z), cosine[d], sine[d])
            q[d, :, lanes] = act.astype(bf16)
            qs[d, :, lanes] = (act * qd[n]).astype(bf16)
            z = k0[d, :, lanes]
            act = turn(z * jax.nn.sigmoid(z), cosine[d], sine[d])
            k[d, :, lanes] = act.astype(bf16)
            scaled = (act * kd[n]).astype(bf16)
            ks[d, :, lanes] = scaled
            local[member ^ d, n] = mm_tn(scaled, v[d, :, lanes])
    for n in range(heads):
        state = jnp.zeros((size, size), f32)
        for b in range(4):
            prefix[b, n] = state
            state = fac[n, 1] * state + local[b, n]
        total[n] = state


def scores_kernel(own, size, q, k, v, mask, w, intra):
    for d in range(4):
        for n in range(own // size):
            lanes = slice(n * size, (n + 1) * size)
            low = (mm_nt(q[d, :, lanes], k[d, :, lanes]) * mask[n]).astype(bf16)
            w[d, n] = low
            intra[d, :, lanes] = mm(low, v[d, :, lanes])


def attend_kernel(own, size, info, fac, prefix, before, qs, intra, u, plow, attn, *z):
    member = info[0]
    for d in range(4):
        b = member ^ d
        for n in range(own // size):
            lanes = slice(n * size, (n + 1) * size)
            low = (prefix[b, n] + fac[n, b] * before[n]).astype(bf16)
            plow[d, n] = low
            a = intra[d, :, lanes] + mm(qs[d, :, lanes], low)
            attn[d, :, lanes] = a
            z[d][:, lanes] = (a * norm_factor(a) * u[d, :, lanes]).astype(bf16)


def mid_kernel(count, block, own, info, x, *refs):
    z, o = refs[:4], refs[4:8]
    y, h2, zp, full, scr = refs[8:]
    member, first = info[0], info[1]
    for d in range(4):
        full[:, pl.ds(pl.multiple_of((member ^ d) * own, own), own)] = z[d][...]
    zp[...] = blocks_of(full, count, block, first)
    mixed = zp[...]
    for d in range(4):
        scr[:, pl.ds(pl.multiple_of((member ^ d) * own, own), own)] = mm(mixed, o[d][...])
    v = x[...].astype(f32) + scr[...]
    y[...] = v
    scr[...] = v * norm_factor(v)
    h2[...] = blocks_of(scr, count, block, first).astype(bf16)


def columns(refs, lo, hi):
    if len(refs) == 1:
        return refs[0][:, lo:hi]
    return jnp.concatenate([r[:, lo:hi] for r in refs], 0)


def columns(refs, lo, hi):
    if len(refs) == 1:
        return refs[0][:, lo:hi]
    return jnp.concatenate([r[:, lo:hi] for r in refs], 0)


def ffn_kernel(wide, h0, h1, c0, c1, *refs):
    h, c, w, outs = (h0, h1), (c0, c1), refs[:-8], refs[-8:]
    for d in range(2):
        hd, dg, df, part = outs[4 * d : 4 * d + 4]
        g = mm(h[d][...], columns(w, 0, wide))
        f = mm(h[d][...], columns(w, wide, 2 * wide))
        hd[...] = (g * f).astype(bf16)
        t = mm(c[d][...], columns(w, 2 * wide, 3 * wide))
        dg[...] = (t * f).astype(bf16)
        df[...] = (t * g).astype(bf16)
        v = mm_nt(dg[...], columns(w, 0, wide)) + mm_nt(df[...], columns(w, wide, 2 * wide))
        part[...] = v.astype(part.dtype)


def ffn_out_kernel(wide, h0, h1, h2, h3, *refs):
    w, outs = refs[:-4], refs[-4:]
    for d, h in enumerate((h0, h1, h2, h3)):
        outs[d][...] = mm_nt(h[...], columns(w, 2 * wide, 3 * wide)).astype(outs[d].dtype)


def store_grads(outs, items, groups, rows, lanes, value):
    half = groups // 2
    for part, one, two in ((0, 1, 2), (1, 2, 1)):
        send, keep2, keep0 = outs[3 * part : 3 * part + 3]
        for i in range(items):
            lo = (i * groups + part * half) * rows
            v = value[lo : lo + half * rows].astype(bf16)
            if i == 0:
                keep0[:, lanes] = v
            elif i == two:
                keep2[:, lanes] = v
            else:
                send[0 if i == one else 1, :, lanes] = v


def hidden_grad_kernel(items, groups, rows, wide, *refs):
    h, dg, df = (refs[4 * n : 4 * n + 4] for n in range(3))
    left = jnp.concatenate([r[...] for r in h], 0)
    for n, right in enumerate((dg, df)):
        value = mm_tn(left, jnp.concatenate([r[...] for r in right], 0))
        store_grads(refs[12:], items, groups, rows, slice(n * wide, (n + 1) * wide), value)


def down_side_kernel(items, groups, rows, wide, own, *refs):
    c, h, hd, du, og, outs = refs[:4], refs[4:8], refs[8:12], refs[12], refs[13:16], refs[16:]
    left = jnp.concatenate([r[...] for r in c], 0)
    value = mm_tn(left, jnp.concatenate([r[...] for r in hd], 0))
    store_grads(outs, items, groups, rows, slice(0, wide), value)
    left = jnp.concatenate([r[...] for r in h], 0)
    value = mm_tn(left, jnp.concatenate([du[d] for d in range(4)], 0))
    store_grads(outs, items, groups, rows, slice(wide, wide + own), value)
    value = og[0][...].astype(f32) + og[1][...].astype(f32) + og[2][...].astype(f32)
    store_grads(outs, items, groups, rows, slice(wide + own, wide + 2 * own), value)


def next_kernel(keep2, got, out):
    out[...] = (keep2[...].astype(f32) + got[1].astype(f32)).astype(bf16)


def sum_kernel(half, *refs):
    parts, outs = (refs[0:3], refs[3:6]), refs[6:]
    rows = outs[0].shape[0]
    for k, out in enumerate(outs):
        keep0, got, far = parts[k // half]
        at = slice((k % half) * rows, (k % half + 1) * rows)
        v = keep0[at].astype(f32) + got[0, at].astype(f32) + far[at].astype(f32)
        out[...] = v.astype(out.dtype)


def add_kernel(keep, got, out):
    out[...] = (keep[...] + got[...].astype(f32)).astype(bf16)


def split_kernel(pieces, info, *refs):
    outs = refs[-4:]
    member = info[0]
    rows = outs[0].shape[0]
    lo = 0
    while len(refs) > 4:
        total, away = refs[0], refs[1:pieces]
        refs = refs[pieces:]
        cols = slice(lo, lo + total.shape[1])
        lo += total.shape[1]
        for d in range(4):
            at = pl.ds(pl.multiple_of((member ^ d) * rows, rows), rows)
            v = total[at, :]
            for r in away:
                v = v + r[at, :].astype(f32)
            outs[d][:, cols] = v.astype(outs[d].dtype)


def mid_back_kernel(count, block, own, info, y, cot, a0, a1, a2, *refs):
    o = refs[:4]
    dy, do, z0, z1, z2, z3, scr = refs[4:]
    z = (z0, z1, z2, z3)
    member, first = info[0], info[1]
    scr[...] = a0[...] + a1[...].astype(f32) + a2[...].astype(f32)
    grad = blocks_of(scr, count, block, first)
    v = y[...]
    scale = norm_factor(v)
    v = cot[...].astype(f32) + norm_back(v * scale, scale, grad)
    dy[...] = v
    do[...] = v.astype(bf16)
    total = None
    for d in range(4):
        part = do[:, pl.ds(pl.multiple_of((member ^ d) * own, own), own)]
        t = mm_nt(part, o[d][...])
        total = t if total is None else total + t
    scr[...] = total
    scr[...] = blocks_of(scr, count, block, first)
    for d in range(4):
        z[d][...] = scr[:, pl.ds(pl.multiple_of((member ^ d) * own, own), own)].astype(bf16)


def out_grad_kernel(own, info, zp, do, *outs):
    member = info[0]
    left = zp[...].T
    for d in range(4):
        part = do[:, pl.ds(pl.multiple_of((member ^ d) * own, own), own)]
        outs[d][...] = mm(left, part).astype(outs[d].dtype)


def back_state_kernel(own, size, info, fac, z0, z1, z2, z3, attn, u, qs, du, da, suffix, total, local):
    member = info[0]
    z = (z0, z1, z2, z3)
    heads = own // size
    for d in range(4):
        for n in range(heads):
            lanes = slice(n * size, (n + 1) * size)
            dz = z[d][:, lanes].astype(f32)
            a = attn[d, :, lanes]
            scale = norm_factor(a)
            normed = a * scale
            du[d, :, lanes] = (dz * normed).astype(bf16)
            low = norm_back(normed, scale, dz * u[d, :, lanes]).astype(bf16)
            da[d, :, lanes] = low
            local[member ^ d, n] = mm_tn(qs[d, :, lanes], low)
    for n in range(heads):
        state = jnp.zeros((size, size), f32)
        for b in (3, 2, 1, 0):
            suffix[b, n] = state
            state = fac[n, 1] * state + local[b, n]
        total[n] = state


def back_local_kernel(own, size, da, v, w, q, k, plow, mask, qd, dq, dk, dv):
    for d in range(4):
        for n in range(own // size):
            lanes = slice(n * size, (n + 1) * size)
            a = da[d, :, lanes]
            ds = (mm_nt(a, v[d, :, lanes]) * mask[n]).astype(bf16)
            dq[d, :, lanes] = mm(ds, k[d, :, lanes]) + mm_nt(a, plow[d, n]) * qd[n]
            dk[d, :, lanes] = mm_tn(ds, q[d, :, lanes])
            dv[d, :, lanes] = mm_tn(w[d, n], a)


def back_final_kernel(nw, own, size, info, fac, suffix, after, v, ks, du, dq, dk, dv, q0, k0, cosine, sine, kd, *refs):
    w, outs = refs[:nw], refs[nw:]
    grads = outs[0]
    parts = outs[1:]
    member = info[0]
    for d in range(4):
        b = member ^ d
        for n in range(own // size):
            lanes = slice(n * size, (n + 1) * size)
            low = (suffix[b, n] + fac[n, 3 - b] * after[n]).astype(bf16)
            dka = dk[d, :, lanes] + mm_nt(v[d, :, lanes], low) * kd[n]
            dvv = dv[d, :, lanes] + mm(ks[d, :, lanes], low)
            z = q0[d, :, lanes]
            s = jax.nn.sigmoid(z)
            g = turn(dq[d, :, lanes], cosine[d], -sine[d]) * s * (1.0 + z * (1.0 - s))
            grads[d, :, n * size : (n + 1) * size] = g.astype(bf16)
            z = k0[d, :, lanes]
            s = jax.nn.sigmoid(z)
            g = turn(dka, cosine[d], -sine[d]) * s * (1.0 + z * (1.0 - s))
            grads[d, :, own + n * size : own + (n + 1) * size] = g.astype(bf16)
            grads[d, :, 2 * own + n * size : 2 * own + (n + 1) * size] = dvv.astype(bf16)
        grads[d, :, 3 * own :] = du[d]
        weights = jnp.concatenate([r[:, : 4 * own] for r in w], 0)
        parts[d][...] = mm_nt(grads[d], weights).astype(parts[d].dtype)


def attn_grad_kernel(items, groups, rows, wide, h0, h1, h2, h3, grads, *outs):
    left = jnp.concatenate([h0[...], h1[...], h2[...], h3[...]], 0)
    value = mm_tn(left, jnp.concatenate([grads[d][:, :wide] for d in range(4)], 0))
    store_grads(outs, items, groups, rows, slice(0, wide), value)


def first_back_kernel(count, block, info, x, dy, a0, a1, a2, out, scr):
    scr[...] = a0[...] + a1[...].astype(f32) + a2[...].astype(f32)
    grad = blocks_of(scr, count, block, info[1])
    v = x[...].astype(f32)
    scale = norm_factor(v)
    out[...] = dy[...] + norm_back(v * scale, scale, grad)


def mixed_kernel(count, block, info, y, a0, a1, a2, out, scr):
    scr[...] = a0[...] + a1[...].astype(f32) + a2[...].astype(f32)
    out[...] = (y[...] + blocks_of(scr, count, block, info[1])).astype(bf16)


def final_kernel(widths, own_cols, info, p0, p1, p2, p3, *outs):
    member = info[0]
    parts = (p0, p1, p2, p3)
    for m in range(4):

        @pl.when(member == m)
        def _():
            for d in range(4):
                j = m ^ d
                lo = 0
                for out, wide, cols in zip(outs, widths, own_cols):
                    out[:, j * cols : (j + 1) * cols] = parts[d][:, lo : lo + cols].astype(f32)
                    lo += wide


def scatter_split(at, info, aligned, sums):
    if aligned:
        rows = sums[0][0].shape[0] // 4
        cols = sum(v[0].shape[1] for v in sums)
        parts = run(
            "split",
            functools.partial(split_kernel, len(sums[0])),
            [like((rows, cols), f32)] + [like((rows, cols), bf16)] * 3,
            [info],
            [v for group in sums for v in group],
        )
    else:
        total = jnp.concatenate([sum(v.astype(f32) for v in group) for group in sums], 1)
        rows = total.shape[0] // 4
        parts = [
            lax.dynamic_slice_in_dim(total, (at.member ^ d) * rows, rows, 0) for d in range(4)
        ]
        parts = [parts[0]] + [v.astype(bf16) for v in parts[1:]]
    return at.exchange(parts)


def rotation_tables(positions, head_size):
    half_width = head_size // 2
    pair_index = jnp.arange(half_width, dtype=jnp.int32)
    step_sizes = jnp.right_shift(jnp.full((half_width,), 8192, jnp.int32), pair_index // 5)
    phase_int = positions[:, None] * step_sizes[None, :] % 65536
    angles = phase_int.astype(f32) * (2.0 * math.pi / 65536.0)
    return (jnp.cos(angles), jnp.sin(angles))


def make_body(items, seqs):
    def body(
        tokens,
        decay_rate,
        query_weight,
        key_weight,
        value_weight,
        update_weight,
        output_weight,
        gate_weight,
        up_weight,
        down_weight,
        cotangent,
    ):
        at = Place(items, seqs)
        groups = at.groups
        width = tokens.shape[-1]
        rows = tokens.shape[1]
        heads = decay_rate.shape[0]
        size = width // heads
        own_heads = heads // 4
        own = width // 4
        shard = query_weight.shape[0]
        hidden = gate_weight.shape[1] // 4
        wide = hidden + -hidden % 256
        count, block = items * groups, 4 * shard
        first = at.item * groups + at.group
        aligned = block % 128 == 0
        if aligned:
            info = jnp.stack([at.member, first])
            kcount, kblock = count, block
        else:
            info = jnp.stack([at.member, jnp.zeros_like(first)])
            kcount, kblock = 1, width
        info = info.astype(jnp.int32)

        def arrange(pieces):
            if aligned:
                return pieces
            v = jnp.stack(pieces)
            return [v[jnp.arange(count) ^ first].reshape(width, -1)]

        def act(dtype=bf16):
            return like((rows, width), dtype)

        blk = functools.partial(like, (4, rows, own))
        x = tokens.reshape(rows, width)
        cot = cotangent.reshape(rows, width)

        half = groups // 2
        packed = pl.pallas_call(
            functools.partial(pack_kernel, own, hidden, wide),
            out_shape=[like((shard, 5 * own + 3 * wide), bf16)] * 4,
            in_specs=[pl.BlockSpec(memory_space=pltpu.SMEM)]
            + [pl.BlockSpec(memory_space=pltpu.HBM)] * 8,
            out_specs=[pl.BlockSpec(memory_space=pltpu.VMEM)] * 4,
            scratch_shapes=[
                pltpu.VMEM((5, shard, width), bf16),
                pltpu.VMEM((3, shard, 4 * hidden), bf16),
                pltpu.SemaphoreType.DMA((8,)),
            ],
            compiler_params=pltpu.CompilerParams(vmem_limit_bytes=56 * MIB),
            cost_estimate=pl.CostEstimate(flops=0, bytes_accessed=0, transcendentals=0),
            name="pack",
        )(
            info,
            query_weight,
            key_weight,
            value_weight,
            update_weight,
            output_weight,
            gate_weight,
            up_weight,
            down_weight.T,
        )
        packed = at.exchange(packed)
        aw = at.in_order([v[:, : 5 * own] for v in packed])
        fw = at.in_order([v[:, 5 * own :] for v in packed])
        near = [aw] + [at.group_swap(aw, k) for k in range(1, groups)]


        def sides(piece, kk):
            one, two = (1, 2) if kk < half else (2, 1)
            return {one: at.item_swap(piece, one), two: at.item_swap(piece, two)}

        def corner(got, kk, after=()):
            one, two = (1, 2) if kk < half else (2, 1)
            if after:
                got[one] = tie(got[one], *after)
            got[3] = at.item_swap(got[one], two)
            return got

        attn_p = [corner(sides(near[k], k), k) for k in range(groups)]
        h1_own, cot_own = run(
            "prep",
            functools.partial(prep_kernel, kcount, kblock),
            [act(), act()],
            [info],
            [x, cot],
            [pltpu.VMEM((rows, width), f32)],
        )
        h1_own = tie(h1_own, aw)
        h1_far = at.swap(h1_own, 2)
        fw = tie(fw, attn_p[0][1], attn_p[0][2], near[-1], h1_far)
        h1 = [h1_own, at.swap(h1_own, 1), h1_far, at.swap(h1_far, 1)]
        far_f = [fw] + [at.group_swap(fw, k) for k in range(1, groups)]
        ffn_p = [sides(far_f[k], k) for k in range(half)]
        early = far_f[1:] + [v for got in ffn_p for v in got.values()]
        attn_w = arrange([near[k] if i == 0 else attn_p[k][i] for i in range(items) for k in range(groups)])
        nw = len(attn_w)

        blocks = at.group * 4 + (at.member ^ jnp.arange(4, dtype=jnp.int32))
        positions = (blocks[:, None] * rows + jnp.arange(rows, dtype=jnp.int32)).reshape(-1)
        cosine, sine = rotation_tables(positions, size)
        cosine = jnp.concatenate([cosine, cosine], 1).reshape(4, rows, size)
        sine = jnp.concatenate([-sine, sine], 1).reshape(4, rows, size)
        log_decay = lax.dynamic_slice(jnp.log(decay_rate), (at.member * own_heads,), (own_heads,))
        local = jnp.arange(rows).astype(f32)
        ld = log_decay[:, None]
        query_decay = jnp.broadcast_to(
            jnp.exp(ld * (local + 1.0))[:, :, None], (own_heads, rows, size)
        )
        key_decay = jnp.broadcast_to(
            jnp.exp(ld * (rows - 1.0 - local))[:, :, None], (own_heads, rows, size)
        )
        offset = local[:, None] - local[None, :]
        mask = jnp.where(
            offset >= 0.0, jnp.exp(log_decay[:, None, None] * jnp.maximum(offset, 0.0)), 0.0
        )
        fac = jnp.exp(ld * rows * jnp.arange(4).astype(f32))
        group_fac = jnp.exp(log_decay * (4.0 * rows))[:, None, None]

        state = like((own_heads, size, size), f32)
        states = like((4, own_heads, size, size), f32)
        states_low = like((4, own_heads, size, size), bf16)
        scratch_states = pltpu.VMEM((4, own_heads, size, size), f32)

        def carried(total, sign):
            out = at.group_shift(total, sign)
            weight = group_fac
            for k in range(2, groups):
                out = out + weight * at.group_shift(total, sign * k)
                weight = weight * group_fac
            return out

        q0, k0, u, v, q, k, qs, ks, prefix, total, out_w = run(
            "project",
            functools.partial(project_kernel, nw, own, size),
            [blk(f32), blk(f32), blk(f32)] + [blk(bf16)] * 5 + [states, state, like((width, own), bf16)],
            [info, fac],
            h1 + attn_w + [cosine, sine, query_decay, key_decay],
            [scratch_states],
            after=early,
            flops=8 * rows * width * 4 * own,
            vmem=VM[0],
        )
        before = carried(total, 1)
        out_far = at.swap(out_w, 2)
        out_core = at.swap(out_w, 1)
        cot_own = tie(cot_own, prefix)
        cot_far = at.swap(cot_own, 2)
        w, intra = run(
            "scores",
            functools.partial(scores_kernel, own, size),
            [like((4, own_heads, rows, rows), bf16), blk(f32)],
            [],
            [q, k, v, mask],
            flops=16 * rows * rows * own,
        )
        plow, attn, *z = run(
            "attend",
            functools.partial(attend_kernel, own, size),
            [states_low, blk(f32)] + [like((rows, own), bf16)] * 4,
            [info, fac],
            [prefix, before, qs, intra, u],
            flops=8 * rows * size * own,
            after=[out_core],
        )
        z = at.exchange(z)
        out_far = tie(out_far, attn)
        out_w = [out_w, out_core, out_far, at.swap(out_far, 1)]
        for kk in range(half, groups):
            far_f[kk] = tie(far_f[kk], prefix)
            ffn_p.append(sides(far_f[kk], kk))
        y, h2_own, zp = run(
            "mid",
            functools.partial(mid_kernel, kcount, kblock, own),
            [act(f32), act(), act()],
            [info],
            [x] + z + out_w,
            [pltpu.VMEM((rows, width), bf16), pltpu.VMEM((rows, width), f32)],
            flops=2 * rows * width * width,
            after=[v for got in ffn_p[half:] for v in got.values()],
        )
        cot_far = tie(cot_far, y)
        cots = [cot_own, at.swap(cot_own, 1), cot_far, at.swap(cot_far, 1)]
        h2 = at.spread(h2_own)
        for kk in range(groups):
            corner(ffn_p[kk], kk, [y])
        ffn_w = arrange(
            [far_f[kk] if i == 0 else ffn_p[kk][i] for i in range(items) for kk in range(groups)]
        )

        hid = like((rows, wide), bf16)
        def gated(a, b, after):
            return run(
                "ffn%d" % a,
                functools.partial(ffn_kernel, wide),
                [hid] * 3 + [act(f32)] + [hid] * 3 + [act()],
                [],
                [h2[a], h2[b], cots[a], cots[b]] + ffn_w,
                vmem=VM[1],
                after=after,
            )

        late = gated(2, 3, [])
        added, mid_far = at.collect_far(late[3], late[7])
        soon = gated(0, 1, [added])
        hd, dg, df = ([soon[n], soon[4 + n], late[n], late[4 + n]] for n in range(3))
        mid_sums = [soon[3], at.swap(soon[7], 1), mid_far]

        def item_blocks(g):
            g = g.astype(bf16).reshape(count, block, -1)[jnp.arange(count) ^ first]
            g = g.reshape(items, groups * block, -1)
            return [g[i] for i in range(items)]

        def halves(g):
            g = item_blocks(g)
            res = []
            for p, one, two in ((0, 1, 2), (1, 2, 1)):
                t = [v[p * half * block : (p + 1) * half * block] for v in g]
                res += [jnp.stack([t[one], t[3]]), t[two], t[0]]
            return res

        def grad_outs(cols):
            return [
                like((2, half * block, cols), bf16),
                like((half * block, cols), bf16),
                like((half * block, cols), bf16),
            ] * 2

        def first_hop(outs):
            return [at.item_swap(outs[0], 1), at.item_swap(outs[3], 2)]

        def second_hop(outs, got, after=()):
            res = []
            for p, two in ((0, 2), (1, 1)):
                keep2, keep0 = outs[3 * p + 1 : 3 * p + 3]
                (v,) = run(
                    "next", next_kernel, [like(keep2.shape, bf16)], [], [keep2, got[p]], after=after
                )
                res += [keep0, got[p], at.item_swap(v, two)]
            return res

        def third_hop(parts, after=()):
            cols = parts[0].shape[1]
            res = run(
                "sum",
                functools.partial(sum_kernel, half),
                [like((block, cols), f32)] + [like((block, cols), bf16)] * (groups - 1),
                [],
                parts,
                after=after,
            )
            return [res[0]] + [at.group_swap(res[k], k) for k in range(1, groups)]

        if aligned:
            hidden_outs = run(
                "hidden_grad",
                functools.partial(hidden_grad_kernel, items, groups, block, wide),
                grad_outs(2 * wide),
                [],
                h2 + dg + df,
                vmem=VM[2],
            )
        else:
            both = [jnp.concatenate(dg, 0), jnp.concatenate(df, 0)]
            hidden_outs = halves(
                jnp.concatenate([mm_tn(jnp.concatenate(h2, 0), v) for v in both], 1)
            )
        hidden_got = first_hop(hidden_outs)

        dy, do, *dz = run(
            "mid_back",
            functools.partial(mid_back_kernel, kcount, kblock, own),
            [act(f32), act()] + [like((rows, own), bf16)] * 4,
            [info],
            [y, cot] + mid_sums + out_w,
            [pltpu.VMEM((rows, width), f32)],
            flops=2 * rows * width * width,
            after=[hidden_outs[0]],
        )
        dz = at.exchange(dz)
        ffn_parts = run(
            "ffn_out",
            functools.partial(ffn_out_kernel, wide),
            [act(f32), act(), act(f32), act()],
            [],
            hd + ffn_w,
            flops=8 * rows * width * wide,
            vmem=VM[3],
        )
        out_sums = at.collect(*ffn_parts)

        og = run(
            "out_grad",
            functools.partial(out_grad_kernel, own),
            [like((width, own), f32), like((width, own), bf16)] * 2,
            [info],
            [zp, do],
            flops=2 * rows * width * width,
        )

        du, da, suffix, gtotal = run(
            "back_state",
            functools.partial(back_state_kernel, own, size),
            [blk(bf16), blk(bf16), states, state],
            [info, fac],
            dz + [attn, u, qs],
            [scratch_states],
            flops=8 * rows * size * own,
            after=[ffn_parts[0]],
        )
        after = carried(gtotal, -1)
        og = at.collect(*og, after=[du])
        hidden_parts = second_hop(hidden_outs, hidden_got, [du])
        dq, dk, dv = run(
            "back_local",
            functools.partial(back_local_kernel, own, size),
            [blk(f32)] * 3,
            [],
            [da, v, w, q, k, plow, mask, query_decay],
            flops=40 * rows * rows * own,
        )
        if aligned:
            ds_outs = run(
                "down_side",
                functools.partial(down_side_kernel, items, groups, block, wide, own),
                grad_outs(wide + 2 * own),
                [],
                cots + h1 + hd + [du] + og,
                flops=8 * rows * width * (wide + own),
                vmem=VM[2],
                after=[dq],
            )
        else:
            hh, cc = jnp.concatenate(h1, 0), jnp.concatenate(cots, 0)
            both = [
                mm_tn(cc, jnp.concatenate(hd, 0)),
                mm_tn(hh, du.reshape(4 * rows, own)),
                sum(v.astype(f32) for v in og),
            ]
            ds_outs = halves(jnp.concatenate(both, 1))
        ds_got = first_hop(ds_outs)
        grads, *part = run(
            "back_final",
            functools.partial(back_final_kernel, nw, own, size),
            [like((4, rows, 4 * own), bf16), act(f32), act(), act(f32), act()],
            [info, fac],
            [suffix, after, v, ks, du, dq, dk, dv, q0, k0, cosine, sine, key_decay] + attn_w,
            flops=8 * rows * width * 4 * own,
            vmem=VM[0],
        )
        if aligned:
            attn_outs = run(
                "attn_grad",
                functools.partial(attn_grad_kernel, items, groups, block, 3 * own),
                grad_outs(3 * own),
                [],
                h1 + [grads],
                flops=6 * rows * width * 4 * own,
                vmem=VM[2],
                after=[hidden_parts[2], hidden_parts[5]],
            )
        else:
            attn_outs = halves(mm_tn(hh, grads[:, :, : 3 * own].reshape(4 * rows, 3 * own)))
        attn_got = first_hop(attn_outs)
        in_sums = at.collect(*part)
        hidden_sums = third_hop(hidden_parts)
        ds_sums = third_hop(second_hop(ds_outs, ds_got, [attn_outs[0], hidden_sums[-1]]))
        attn_sums = third_hop(second_hop(attn_outs, attn_got))
        hidden_own = scatter_split(at, info, aligned, [hidden_sums])
        rest_own = scatter_split(at, info, aligned, [attn_sums, ds_sums])
        (mixed,) = run(
            "mixed",
            functools.partial(mixed_kernel, kcount, kblock),
            [act()],
            [info],
            [y] + out_sums,
            [pltpu.VMEM((rows, width), f32)],
            after=[attn_outs[0]],
        )
        tokens_grad = run(
            "first_back",
            functools.partial(first_back_kernel, kcount, kblock),
            [act(f32)],
            [info],
            [x, dy] + in_sums,
            [pltpu.VMEM((rows, width), f32)],
        )[0]
        gg, pg = run(
            "final_hidden",
            functools.partial(final_kernel, (wide,) * 2, (hidden,) * 2),
            [like((shard, 4 * hidden), f32)] * 2,
            [info],
            hidden_own,
        )
        qg, kg, vg, ng, ug, wg = run(
            "final_rest",
            functools.partial(
                final_kernel, (own,) * 3 + (wide,) + (own,) * 2, (own,) * 3 + (hidden,) + (own,) * 2
            ),
            [like((shard, width), f32)] * 3
            + [like((shard, 4 * hidden), f32)]
            + [like((shard, width), f32)] * 2,
            [info],
            rest_own,
        )
        return (
            mixed.reshape(tokens.shape),
            tokens_grad.reshape(tokens.shape),
            qg,
            kg,
            vg,
            ug,
            wg,
            gg,
            pg,
            ng.T,
        )

    return body


def solution(mesh):
    items, seqs = mesh.shape["items"], mesh.shape["seq"]
    parts = jax.sharding.Mesh(mesh.devices.reshape(items, seqs // 4, 4), AXES)
    act = P("items", ("group", "member"), None)
    row = P(AXES, None)
    col = P(None, AXES)
    return jax.shard_map(
        make_body(items, seqs),
        mesh=parts,
        in_specs=(act, P()) + (row,) * 7 + (col, act),
        out_specs=(act, act) + (row,) * 7 + (col,),
        check_vma=False,
    )
```

```python
import functools
import math

import jax
import jax.numpy as jnp
from jax import lax
from jax.experimental import pallas as pl
from jax.experimental.pallas import tpu as pltpu
from jax.sharding import PartitionSpec as P

epsilon = 1e-06
AXES = ("items", "group", "member")
f32 = jnp.float32
bf16 = jnp.bfloat16
MIB = 1024 * 1024
VM = (12, 16, 16, 16)
WEIGHT = {}


def mm(a, b):
    return jnp.dot(a, b, preferred_element_type=f32)


def mm_tn(a, b):
    return lax.dot_general(a, b, (((0,), (0,)), ((), ())), preferred_element_type=f32)


def mm_nt(a, b):
    return lax.dot_general(a, b, (((1,), (1,)), ((), ())), preferred_element_type=f32)


def norm_factor(v):
    return lax.rsqrt(jnp.mean(v * v, axis=-1, keepdims=True) + epsilon)


def norm_back(normed, scale, grad):
    return scale * (grad - normed * jnp.mean(grad * normed, axis=-1, keepdims=True))


def like(shape, dtype):
    return jax.ShapeDtypeStruct(tuple(shape), dtype)


def run(name, kernel, outs, scalars, arrays, scratch=(), flops=0, vmem=10, after=(), alias=None):
    ins = list(scalars) + list(arrays) + list(after)
    used, held = len(scalars) + len(arrays), len(after)

    def body(*refs):
        kernel(*refs[:used], *refs[used + held :])

    size = sum(v.size * v.dtype.itemsize for v in list(arrays) + list(outs)) if flops else 0
    size, flops = (int(v * WEIGHT.get(name, 1)) for v in (size, flops))
    return pl.pallas_call(
        body,
        out_shape=list(outs),
        in_specs=[pl.BlockSpec(memory_space=pltpu.SMEM)] * len(scalars)
        + [pl.BlockSpec(memory_space=pltpu.VMEM)] * len(arrays)
        + [pl.BlockSpec(memory_space=pl.ANY)] * held,
        out_specs=[pl.BlockSpec(memory_space=pltpu.VMEM)] * len(outs),
        scratch_shapes=list(scratch),
        input_output_aliases=alias or {},
        compiler_params=pltpu.CompilerParams(vmem_limit_bytes=vmem * MIB),
        cost_estimate=pl.CostEstimate(flops=flops, bytes_accessed=size, transcendentals=0),
        name=name,
    )(*ins)


def tie(v, *after):
    anywhere = pl.BlockSpec(memory_space=pl.ANY)
    return pl.pallas_call(
        lambda *refs: None,
        out_shape=like(v.shape, v.dtype),
        in_specs=[anywhere] * (1 + len(after)),
        out_specs=anywhere,
        input_output_aliases={0: 0},
        compiler_params=pltpu.CompilerParams(vmem_limit_bytes=MIB),
        name="tie",
        cost_estimate=pl.CostEstimate(flops=0, bytes_accessed=0, transcendentals=0),
    )(v, *after)


class Place:
    def __init__(self, items, seqs):
        self.items, self.seqs, self.groups = items, seqs, seqs // 4
        self.count = items * seqs
        self.item, self.group, self.member = (lax.axis_index(name) for name in AXES)

    def swap(self, v, mask):
        return lax.ppermute(v, AXES, [(d, d ^ mask) for d in range(self.count)])

    def group_swap(self, v, k):
        return self.swap(v, 4 * k)

    def item_swap(self, v, k):
        return self.swap(v, self.seqs * k)

    def group_shift(self, v, k):
        pairs = []
        for d in range(self.count):
            g = (d % self.seqs) // 4 + k
            if 0 <= g < self.groups:
                pairs.append((d, d + 4 * k))
        return lax.ppermute(v, AXES, pairs)

    def spread(self, v):
        far = self.swap(v, 2)
        return [v, self.swap(v, 1), far, self.swap(far, 1)]

    def exchange(self, parts):
        return [parts[0]] + [self.swap(parts[d], d) for d in (1, 2, 3)]

    def collect_far(self, keep2, send3, after=()):
        pair = [keep2, self.swap(send3, 1)]
        (v,) = run("add", add_kernel, [like(keep2.shape, bf16)], [], pair, after=after)
        return v, self.swap(v, 2)

    def collect(self, keep0, send1, keep2, send3, after=()):
        far = self.collect_far(keep2, send3, after)[1]
        return [keep0, self.swap(send1, 1), far]

    def in_order(self, parts):
        out = None
        for m in (3, 2, 1, 0):
            v = jnp.concatenate([parts[m ^ k] for k in range(4)], 0)
            out = v if out is None else jnp.where(self.member == m, v, out)
        return out


def blocks_of(ref, count, size, first):
    if count == 1:
        return ref[...]
    return jnp.concatenate(
        [ref[:, pl.ds(pl.multiple_of((k ^ first) * size, size), size)] for k in range(count)], 1
    )


def rows_of(refs):
    if len(refs) == 1:
        return refs[0][...]
    return jnp.concatenate([r[...] for r in refs], 0)


def pack_kernel(own, hidden, wide, info, q, k, v, u, o, g, up, dn, *refs):
    outs, wides, small, large, sems = refs[:4], refs[4:8], refs[8], refs[9], refs[10]
    copies = [
        pltpu.make_async_copy(ref, small.at[n], sems.at[n]) for n, ref in enumerate((q, k, v, u, o))
    ] + [pltpu.make_async_copy(ref, large.at[n], sems.at[5 + n]) for n, ref in enumerate((g, up, dn))]
    for copy in copies:
        copy.start()
    for copy in copies:
        copy.wait()
    member = info[0]
    for m in range(4):

        @pl.when(member == m)
        def _():
            for d in range(4):
                j = m ^ d
                for n in range(5):
                    outs[d][:, n * own : (n + 1) * own] = small[n, :, j * own : (j + 1) * own]
                for n in range(3):
                    v = large[n, :, j * hidden : (j + 1) * hidden]
                    if wide != hidden:
                        v = jnp.concatenate(
                            [v, jnp.zeros((v.shape[0], wide - hidden), v.dtype)], 1
                        )
                    wides[d][:, n * wide : (n + 1) * wide] = v


def prep_kernel(count, block, info, x, c, h_out, c_out, scr):
    first = info[1]
    v = x[...].astype(f32)
    scr[...] = v * norm_factor(v)
    h_out[...] = blocks_of(scr, count, block, first).astype(bf16)
    scr[...] = c[...].astype(f32)
    c_out[...] = blocks_of(scr, count, block, first).astype(bf16)


def turn(v, cosine, sine):
    return v * cosine + pltpu.roll(v, v.shape[-1] // 2, 1) * sine


def project_kernel(nw, own, size, info, fac, *refs):
    h, w = refs[:4], refs[4 : 4 + nw]
    cosine, sine, qd, kd = refs[4 + nw : 8 + nw]
    q0, k0, u, v, q, k, qs, ks, prefix, total, out_w, local = refs[8 + nw :]
    member = info[0]
    out_w[...] = jnp.concatenate([r[:, 4 * own :] for r in w], 0)
    heads = own // size
    for d in range(4):
        weights = jnp.concatenate([r[:, : 4 * own] for r in w], 0)
        pre = mm(h[d][...], weights)
        q0[d] = pre[:, :own]
        k0[d] = pre[:, own : 2 * own]
        v[d] = pre[:, 2 * own : 3 * own].astype(bf16)
        u[d] = pre[:, 3 * own :]
        for n in range(heads):
            lanes = slice(n * size, (n + 1) * size)
            z = q0[d, :, lanes]
            act = turn(z * jax.nn.sigmoid(z), cosine[d], sine[d])
            q[d, :, lanes] = act.astype(bf16)
            qs[d, :, lanes] = (act * qd[n]).astype(bf16)
            z = k0[d, :, lanes]
            act = turn(z * jax.nn.sigmoid(z), cosine[d], sine[d])
            k[d, :, lanes] = act.astype(bf16)
            scaled = (act * kd[n]).astype(bf16)
            ks[d, :, lanes] = scaled
            local[member ^ d, n] = mm_tn(scaled, v[d, :, lanes])
    for n in range(heads):
        state = jnp.zeros((size, size), f32)
        for b in range(4):
            prefix[b, n] = state
            state = fac[n, 1] * state + local[b, n]
        total[n] = state


def scores_kernel(own, size, q, k, v, mask, w, intra):
    for d in range(4):
        for n in range(own // size):
            lanes = slice(n * size, (n + 1) * size)
            low = (mm_nt(q[d, :, lanes], k[d, :, lanes]) * mask[n]).astype(bf16)
            w[d, n] = low
            intra[d, :, lanes] = mm(low, v[d, :, lanes])


def attend_kernel(own, size, info, fac, prefix, before, qs, intra, u, plow, attn, *z):
    member = info[0]
    for d in range(4):
        b = member ^ d
        for n in range(own // size):
            lanes = slice(n * size, (n + 1) * size)
            low = (prefix[b, n] + fac[n, b] * before[n]).astype(bf16)
            plow[d, n] = low
            a = intra[d, :, lanes] + mm(qs[d, :, lanes], low)
            attn[d, :, lanes] = a
            z[d][:, lanes] = (a * norm_factor(a) * u[d, :, lanes]).astype(bf16)


def mid_kernel(count, block, own, info, x, *refs):
    z, o = refs[:4], refs[4:8]
    y, h2, zp, full, scr = refs[8:]
    member, first = info[0], info[1]
    for d in range(4):
        full[:, pl.ds(pl.multiple_of((member ^ d) * own, own), own)] = z[d][...]
    zp[...] = blocks_of(full, count, block, first)
    mixed = zp[...]
    for d in range(4):
        scr[:, pl.ds(pl.multiple_of((member ^ d) * own, own), own)] = mm(mixed, o[d][...])
    v = x[...].astype(f32) + scr[...]
    y[...] = v
    scr[...] = v * norm_factor(v)
    h2[...] = blocks_of(scr, count, block, first).astype(bf16)


def columns(refs, lo, hi):
    if len(refs) == 1:
        return refs[0][:, lo:hi]
    return jnp.concatenate([r[:, lo:hi] for r in refs], 0)


def columns(refs, lo, hi):
    if len(refs) == 1:
        return refs[0][:, lo:hi]
    return jnp.concatenate([r[:, lo:hi] for r in refs], 0)


def ffn_kernel(wide, h0, h1, c0, c1, *refs):
    h, c, w, outs = (h0, h1), (c0, c1), refs[:-8], refs[-8:]
    for d in range(2):
        hd, dg, df, part = outs[4 * d : 4 * d + 4]
        g = mm(h[d][...], columns(w, 0, wide))
        f = mm(h[d][...], columns(w, wide, 2 * wide))
        hd[...] = (g * f).astype(bf16)
        t = mm(c[d][...], columns(w, 2 * wide, 3 * wide))
        dg[...] = (t * f).astype(bf16)
        df[...] = (t * g).astype(bf16)
        v = mm_nt(dg[...], columns(w, 0, wide)) + mm_nt(df[...], columns(w, wide, 2 * wide))
        part[...] = v.astype(part.dtype)


def ffn_out_kernel(wide, h0, h1, h2, h3, *refs):
    w, outs = refs[:-4], refs[-4:]
    for d, h in enumerate((h0, h1, h2, h3)):
        outs[d][1] = mm_nt(h[...], columns(w, 2 * wide, 3 * wide)).astype(outs[d].dtype)


def store_grads(outs, items, groups, rows, lanes, value):
    half = groups // 2
    for part, one, two in ((0, 1, 2), (1, 2, 1)):
        send, keep2, keep0 = outs[3 * part : 3 * part + 3]
        for i in range(items):
            lo = (i * groups + part * half) * rows
            v = value[lo : lo + half * rows].astype(bf16)
            if i == 0:
                keep0[:, lanes] = v
            elif i == two:
                keep2[:, lanes] = v
            else:
                send[0 if i == one else 1, :, lanes] = v


def hidden_grad_kernel(items, groups, rows, wide, *refs):
    h, dg, df = (refs[4 * n : 4 * n + 4] for n in range(3))
    left = jnp.concatenate([r[...] for r in h], 0)
    for n, right in enumerate((dg, df)):
        value = mm_tn(left, jnp.concatenate([r[...] for r in right], 0))
        store_grads(refs[12:], items, groups, rows, slice(n * wide, (n + 1) * wide), value)


def down_side_kernel(items, groups, rows, wide, own, *refs):
    c, h, hd, dq, du, outs = refs[:4], refs[4:8], refs[8:12], refs[12], refs[13], refs[14:]
    left = jnp.concatenate([r[...] for r in c], 0)
    value = mm_tn(left, jnp.concatenate([r[...] for r in hd], 0))
    store_grads(outs, items, groups, rows, slice(0, wide), value)
    left = jnp.concatenate([r[...] for r in h], 0)
    right = jnp.concatenate([jnp.concatenate([dq[d], du[d]], 1) for d in range(4)], 0)
    store_grads(outs, items, groups, rows, slice(wide, wide + 2 * own), mm_tn(left, right))


def next_kernel(keep2, got, out):
    out[...] = (keep2[...].astype(f32) + got[1].astype(f32)).astype(bf16)


def sum_kernel(half, *refs):
    parts, outs = (refs[0:3], refs[3:6]), refs[6:]
    rows = outs[0].shape[0]
    for k, out in enumerate(outs):
        keep0, got, far = parts[k // half]
        at = slice((k % half) * rows, (k % half + 1) * rows)
        v = keep0[at].astype(f32) + got[0, at].astype(f32) + far[at].astype(f32)
        out[...] = v.astype(out.dtype)


def add_kernel(keep, got, out):
    out[...] = (keep[...] + got[...].astype(f32)).astype(bf16)


def split_kernel(pieces, info, *refs):
    outs = refs[-4:]
    member = info[0]
    rows = outs[0].shape[0]
    lo = 0
    while len(refs) > 4:
        total, away = refs[0], refs[1:pieces]
        refs = refs[pieces:]
        cols = slice(lo, lo + total.shape[1])
        lo += total.shape[1]
        for d in range(4):
            at = pl.ds(pl.multiple_of((member ^ d) * rows, rows), rows)
            v = total[at, :]
            for r in away:
                v = v + r[at, :].astype(f32)
            outs[d][:, cols] = v.astype(outs[d].dtype)


def mid_back_kernel(count, block, own, info, y, cot, a0, a1, a2, *refs):
    o = refs[:4]
    dy, do, z0, z1, z2, z3, scr = refs[4:]
    z = (z0, z1, z2, z3)
    member, first = info[0], info[1]
    scr[...] = a0[...] + a1[...].astype(f32) + a2[...].astype(f32)
    grad = blocks_of(scr, count, block, first)
    v = y[...]
    scale = norm_factor(v)
    v = cot[...].astype(f32) + norm_back(v * scale, scale, grad)
    dy[...] = v
    do[...] = v.astype(bf16)
    total = None
    for d in range(4):
        part = do[:, pl.ds(pl.multiple_of((member ^ d) * own, own), own)]
        t = mm_nt(part, o[d][...])
        total = t if total is None else total + t
    scr[...] = total
    scr[...] = blocks_of(scr, count, block, first)
    for d in range(4):
        z[d][...] = scr[:, pl.ds(pl.multiple_of((member ^ d) * own, own), own)].astype(bf16)


def out_grad_kernel(own, info, zp, do, *outs):
    member = info[0]
    left = zp[...].T
    for d in range(4):
        part = do[:, pl.ds(pl.multiple_of((member ^ d) * own, own), own)]
        outs[d][...] = mm(left, part).astype(outs[d].dtype)


def back_state_kernel(own, size, info, fac, z0, z1, z2, z3, attn, u, qs, du, da, suffix, total, local):
    member = info[0]
    z = (z0, z1, z2, z3)
    heads = own // size
    for d in range(4):
        for n in range(heads):
            lanes = slice(n * size, (n + 1) * size)
            dz = z[d][:, lanes].astype(f32)
            a = attn[d, :, lanes]
            scale = norm_factor(a)
            normed = a * scale
            du[d, :, lanes] = (dz * normed).astype(bf16)
            low = norm_back(normed, scale, dz * u[d, :, lanes]).astype(bf16)
            da[d, :, lanes] = low
            local[member ^ d, n] = mm_tn(qs[d, :, lanes], low)
    for n in range(heads):
        state = jnp.zeros((size, size), f32)
        for b in (3, 2, 1, 0):
            suffix[b, n] = state
            state = fac[n, 1] * state + local[b, n]
        total[n] = state


def back_local_kernel(own, size, da, v, w, q, k, plow, mask, qd, q0, cosine, sine, dq, dk, dv):
    for d in range(4):
        for n in range(own // size):
            lanes = slice(n * size, (n + 1) * size)
            a = da[d, :, lanes]
            ds = (mm_nt(a, v[d, :, lanes]) * mask[n]).astype(bf16)
            g = mm(ds, k[d, :, lanes]) + mm_nt(a, plow[d, n]) * qd[n]
            z = q0[d, :, lanes]
            s = jax.nn.sigmoid(z)
            g = turn(g, cosine[d], -sine[d]) * s * (1.0 + z * (1.0 - s))
            dq[d, :, lanes] = g.astype(bf16)
            dk[d, :, lanes] = mm_tn(ds, q[d, :, lanes])
            dv[d, :, lanes] = mm_tn(w[d, n], a)


def back_final_kernel(nw, own, size, info, fac, suffix, after, v, ks, du, dq, dk, dv, k0, cosine, sine, kd, *refs):
    w, outs = refs[:nw], refs[nw + 4 :]
    grads = outs[0]
    parts = outs[1:]
    member = info[0]
    for d in range(4):
        b = member ^ d
        for n in range(own // size):
            lanes = slice(n * size, (n + 1) * size)
            low = (suffix[b, n] + fac[n, 3 - b] * after[n]).astype(bf16)
            dka = dk[d, :, lanes] + mm_nt(v[d, :, lanes], low) * kd[n]
            dvv = dv[d, :, lanes] + mm(ks[d, :, lanes], low)
            z = k0[d, :, lanes]
            s = jax.nn.sigmoid(z)
            g = turn(dka, cosine[d], -sine[d]) * s * (1.0 + z * (1.0 - s))
            grads[d, :, own + n * size : own + (n + 1) * size] = g.astype(bf16)
            grads[d, :, 2 * own + n * size : 2 * own + (n + 1) * size] = dvv.astype(bf16)
        grads[d, :, :own] = dq[d]
        grads[d, :, 3 * own :] = du[d]
        weights = jnp.concatenate([r[:, : 4 * own] for r in w], 0)
        parts[d][0] = mm_nt(grads[d], weights).astype(parts[d].dtype)


def attn_grad_kernel(items, groups, rows, own, h0, h1, h2, h3, grads, o0, o1, o2, *outs):
    left = jnp.concatenate([h0[...], h1[...], h2[...], h3[...]], 0)
    value = mm_tn(left, jnp.concatenate([grads[d][:, own : 3 * own] for d in range(4)], 0))
    store_grads(outs, items, groups, rows, slice(0, 2 * own), value)
    value = o0[...].astype(f32) + o1[...].astype(f32) + o2[...].astype(f32)
    store_grads(outs, items, groups, rows, slice(2 * own, 3 * own), value)


def first_back_kernel(count, block, info, x, dy, a0, a1, a2, out, scr):
    scr[...] = a0[0] + a1[0].astype(f32) + a2[0].astype(f32)
    grad = blocks_of(scr, count, block, info[1])
    v = x[...].astype(f32)
    scale = norm_factor(v)
    out[...] = dy[...] + norm_back(v * scale, scale, grad)


def mixed_kernel(count, block, info, y, a0, a1, a2, out, scr):
    scr[...] = a0[1] + a1[1].astype(f32) + a2[1].astype(f32)
    out[...] = (y[...] + blocks_of(scr, count, block, info[1])).astype(bf16)


def final_kernel(widths, own_cols, info, p0, p1, p2, p3, *outs):
    member = info[0]
    parts = (p0, p1, p2, p3)
    for m in range(4):

        @pl.when(member == m)
        def _():
            for d in range(4):
                j = m ^ d
                lo = 0
                for out, wide, cols in zip(outs, widths, own_cols):
                    out[:, j * cols : (j + 1) * cols] = parts[d][:, lo : lo + cols].astype(f32)
                    lo += wide


def scatter_split(at, info, aligned, sums, after=()):
    if aligned:
        rows = sums[0][0].shape[0] // 4
        cols = sum(v[0].shape[1] for v in sums)
        parts = run(
            "split",
            functools.partial(split_kernel, len(sums[0])),
            [like((rows, cols), f32)] + [like((rows, cols), bf16)] * 3,
            [info],
            [v for group in sums for v in group],
            after=after,
        )
    else:
        total = jnp.concatenate([sum(v.astype(f32) for v in group) for group in sums], 1)
        rows = total.shape[0] // 4
        parts = [
            lax.dynamic_slice_in_dim(total, (at.member ^ d) * rows, rows, 0) for d in range(4)
        ]
        parts = [parts[0]] + [v.astype(bf16) for v in parts[1:]]
    return at.exchange(parts)


def rotation_tables(positions, head_size):
    half_width = head_size // 2
    pair_index = jnp.arange(half_width, dtype=jnp.int32)
    step_sizes = jnp.right_shift(jnp.full((half_width,), 8192, jnp.int32), pair_index // 5)
    phase_int = positions[:, None] * step_sizes[None, :] % 65536
    angles = phase_int.astype(f32) * (2.0 * math.pi / 65536.0)
    return (jnp.cos(angles), jnp.sin(angles))


def make_body(items, seqs):
    def body(
        tokens,
        decay_rate,
        query_weight,
        key_weight,
        value_weight,
        update_weight,
        output_weight,
        gate_weight,
        up_weight,
        down_weight,
        cotangent,
    ):
        at = Place(items, seqs)
        groups = at.groups
        width = tokens.shape[-1]
        rows = tokens.shape[1]
        heads = decay_rate.shape[0]
        size = width // heads
        own_heads = heads // 4
        own = width // 4
        shard = query_weight.shape[0]
        hidden = gate_weight.shape[1] // 4
        wide = hidden + -hidden % 256
        count, block = items * groups, 4 * shard
        first = at.item * groups + at.group
        aligned = block % 128 == 0
        if aligned:
            info = jnp.stack([at.member, first])
            kcount, kblock = count, block
        else:
            info = jnp.stack([at.member, jnp.zeros_like(first)])
            kcount, kblock = 1, width
        info = info.astype(jnp.int32)

        def arrange(pieces):
            if aligned:
                return pieces
            v = jnp.stack(pieces)
            return [v[jnp.arange(count) ^ first].reshape(width, -1)]

        def act(dtype=bf16):
            return like((rows, width), dtype)

        blk = functools.partial(like, (4, rows, own))
        x = tokens.reshape(rows, width)
        cot = cotangent.reshape(rows, width)

        half = groups // 2
        packed = pl.pallas_call(
            functools.partial(pack_kernel, own, hidden, wide),
            out_shape=[like((shard, 5 * own), bf16)] * 4 + [like((shard, 3 * wide), bf16)] * 4,
            in_specs=[pl.BlockSpec(memory_space=pltpu.SMEM)]
            + [pl.BlockSpec(memory_space=pltpu.HBM)] * 8,
            out_specs=[pl.BlockSpec(memory_space=pltpu.VMEM)] * 8,
            scratch_shapes=[
                pltpu.VMEM((5, shard, width), bf16),
                pltpu.VMEM((3, shard, 4 * hidden), bf16),
                pltpu.SemaphoreType.DMA((8,)),
            ],
            compiler_params=pltpu.CompilerParams(vmem_limit_bytes=56 * MIB),
            cost_estimate=pl.CostEstimate(flops=0, bytes_accessed=0, transcendentals=0),
            name="pack",
        )(
            info,
            query_weight,
            key_weight,
            value_weight,
            update_weight,
            output_weight,
            gate_weight,
            up_weight,
            down_weight.T,
        )
        aw = at.in_order(at.exchange(packed[:4]))
        fw = at.in_order(at.exchange(packed[4:]))
        near = [aw] + [at.group_swap(aw, k) for k in range(1, groups)]


        def sides(piece, kk):
            one, two = (1, 2) if kk < half else (2, 1)
            return {one: at.item_swap(piece, one), two: at.item_swap(piece, two)}

        def corner(got, kk, after=()):
            one, two = (1, 2) if kk < half else (2, 1)
            if after:
                got[one] = tie(got[one], *after)
            got[3] = at.item_swap(got[one], two)
            return got

        attn_p = [corner(sides(near[k], k), k) for k in range(groups)]
        h1_own, cot_own = run(
            "prep",
            functools.partial(prep_kernel, kcount, kblock),
            [act(), act()],
            [info],
            [x, cot],
            [pltpu.VMEM((rows, width), f32)],
        )
        h1_own = tie(h1_own, aw)
        h1_far = at.swap(h1_own, 2)
        fw = tie(fw, attn_p[0][1], attn_p[0][2], near[-1], h1_far)
        h1 = [h1_own, at.swap(h1_own, 1), h1_far, at.swap(h1_far, 1)]
        far_f = [fw] + [at.group_swap(fw, k) for k in range(1, groups)]
        ffn_p = [sides(far_f[k], k) for k in range(half)]
        early = far_f[1:] + [v for got in ffn_p for v in got.values()]
        attn_w = arrange([near[k] if i == 0 else attn_p[k][i] for i in range(items) for k in range(groups)])
        nw = len(attn_w)

        blocks = at.group * 4 + (at.member ^ jnp.arange(4, dtype=jnp.int32))
        positions = (blocks[:, None] * rows + jnp.arange(rows, dtype=jnp.int32)).reshape(-1)
        cosine, sine = rotation_tables(positions, size)
        cosine = jnp.concatenate([cosine, cosine], 1).reshape(4, rows, size)
        sine = jnp.concatenate([-sine, sine], 1).reshape(4, rows, size)
        log_decay = lax.dynamic_slice(jnp.log(decay_rate), (at.member * own_heads,), (own_heads,))
        local = jnp.arange(rows).astype(f32)
        ld = log_decay[:, None]
        query_decay = jnp.broadcast_to(
            jnp.exp(ld * (local + 1.0))[:, :, None], (own_heads, rows, size)
        )
        key_decay = jnp.broadcast_to(
            jnp.exp(ld * (rows - 1.0 - local))[:, :, None], (own_heads, rows, size)
        )
        offset = local[:, None] - local[None, :]
        mask = jnp.where(
            offset >= 0.0, jnp.exp(log_decay[:, None, None] * jnp.maximum(offset, 0.0)), 0.0
        )
        fac = jnp.exp(ld * rows * jnp.arange(4).astype(f32))
        group_fac = jnp.exp(log_decay * (4.0 * rows))[:, None, None]

        state = like((own_heads, size, size), f32)
        states = like((4, own_heads, size, size), f32)
        states_low = like((4, own_heads, size, size), bf16)
        scratch_states = pltpu.VMEM((4, own_heads, size, size), f32)

        def carried(total, sign):
            out = at.group_shift(total, sign)
            weight = group_fac
            for k in range(2, groups):
                out = out + weight * at.group_shift(total, sign * k)
                weight = weight * group_fac
            return out

        q0, k0, u, v, q, k, qs, ks, prefix, total, out_w = run(
            "project",
            functools.partial(project_kernel, nw, own, size),
            [blk(f32), blk(f32), blk(f32)] + [blk(bf16)] * 5 + [states, state, like((width, own), bf16)],
            [info, fac],
            h1 + attn_w + [cosine, sine, query_decay, key_decay],
            [scratch_states],
            after=early,
            flops=8 * rows * width * 4 * own,
            vmem=VM[0],
        )
        before = carried(total, 1)
        out_far = at.swap(out_w, 2)
        out_core = at.swap(out_w, 1)
        cot_own = tie(cot_own, prefix)
        cot_far = at.swap(cot_own, 2)
        w, intra = run(
            "scores",
            functools.partial(scores_kernel, own, size),
            [like((4, own_heads, rows, rows), bf16), blk(f32)],
            [],
            [q, k, v, mask],
            flops=16 * rows * rows * own,
        )
        plow, attn, *z = run(
            "attend",
            functools.partial(attend_kernel, own, size),
            [states_low, blk(f32)] + [like((rows, own), bf16)] * 4,
            [info, fac],
            [prefix, before, qs, intra, u],
            flops=8 * rows * size * own,
            after=[out_core],
        )
        z = at.exchange(z)
        out_far = tie(out_far, attn)
        out_w = [out_w, out_core, out_far, at.swap(out_far, 1)]
        for kk in range(half, groups):
            far_f[kk] = tie(far_f[kk], prefix)
            ffn_p.append(sides(far_f[kk], kk))
        y, h2_own, zp = run(
            "mid",
            functools.partial(mid_kernel, kcount, kblock, own),
            [act(f32), act(), act()],
            [info],
            [x] + z + out_w,
            [pltpu.VMEM((rows, width), bf16), pltpu.VMEM((rows, width), f32)],
            flops=2 * rows * width * width,
            after=[v for got in ffn_p[half:] for v in got.values()],
        )
        cot_far = tie(cot_far, y)
        cots = [cot_own, at.swap(cot_own, 1), cot_far, at.swap(cot_far, 1)]
        h2 = at.spread(h2_own)
        for kk in range(groups):
            corner(ffn_p[kk], kk, [y])
        ffn_w = arrange(
            [far_f[kk] if i == 0 else ffn_p[kk][i] for i in range(items) for kk in range(groups)]
        )

        hid = like((rows, wide), bf16)
        def gated(a, b, after):
            return run(
                "ffn%d" % a,
                functools.partial(ffn_kernel, wide),
                [hid] * 3 + [act(f32)] + [hid] * 3 + [act()],
                [],
                [h2[a], h2[b], cots[a], cots[b]] + ffn_w,
                vmem=VM[1],
                after=after,
            )

        late = gated(2, 3, [])
        added, mid_far = at.collect_far(late[3], late[7])
        soon = gated(0, 1, [added])
        hd, dg, df = ([soon[n], soon[4 + n], late[n], late[4 + n]] for n in range(3))
        mid_sums = [soon[3], at.swap(soon[7], 1), mid_far]

        def item_blocks(g):
            g = g.astype(bf16).reshape(count, block, -1)[jnp.arange(count) ^ first]
            g = g.reshape(items, groups * block, -1)
            return [g[i] for i in range(items)]

        def halves(g):
            g = item_blocks(g)
            res = []
            for p, one, two in ((0, 1, 2), (1, 2, 1)):
                t = [v[p * half * block : (p + 1) * half * block] for v in g]
                res += [jnp.stack([t[one], t[3]]), t[two], t[0]]
            return res

        def grad_outs(cols):
            return [
                like((2, half * block, cols), bf16),
                like((half * block, cols), bf16),
                like((half * block, cols), bf16),
            ] * 2

        def first_hop(outs):
            return [at.item_swap(outs[0], 1), at.item_swap(outs[3], 2)]

        def second_hop(outs, got, after=()):
            res, sent = [], []
            for p, two in ((0, 2), (1, 1)):
                keep2, keep0 = outs[3 * p + 1 : 3 * p + 3]
                (v,) = run(
                    "next", next_kernel, [like(keep2.shape, bf16)], [], [keep2, got[p]], after=after
                )
                res += [keep0, got[p], at.item_swap(v, two)]
                sent.append(v)
            return res, sent

        def third_hop(parts, after=()):
            cols = parts[0].shape[1]
            res = run(
                "sum",
                functools.partial(sum_kernel, half),
                [like((block, cols), f32)] + [like((block, cols), bf16)] * (groups - 1),
                [],
                parts,
                after=after,
            )
            return [res[0]] + [at.group_swap(res[k], k) for k in range(1, groups)]

        if aligned:
            hidden_outs = run(
                "hidden_grad",
                functools.partial(hidden_grad_kernel, items, groups, block, wide),
                grad_outs(2 * wide),
                [],
                h2 + dg + df,
                vmem=VM[2],
            )
        else:
            both = [jnp.concatenate(dg, 0), jnp.concatenate(df, 0)]
            hidden_outs = halves(
                jnp.concatenate([mm_tn(jnp.concatenate(h2, 0), v) for v in both], 1)
            )
        hidden_got = first_hop(hidden_outs)

        dy, do, *dz = run(
            "mid_back",
            functools.partial(mid_back_kernel, kcount, kblock, own),
            [act(f32), act()] + [like((rows, own), bf16)] * 4,
            [info],
            [y, cot] + mid_sums + out_w,
            [pltpu.VMEM((rows, width), f32)],
            flops=2 * rows * width * width,
            after=[hidden_outs[0]],
        )
        dz = at.exchange(dz)
        two_acts = [like((2, rows, width), t) for t in (f32, bf16, f32, bf16)]
        ffn_parts = [None] * 4
        ffn_parts[:] = run(
            "ffn_out",
            functools.partial(ffn_out_kernel, wide),
            two_acts,
            [],
            hd + ffn_w,
            flops=8 * rows * width * wide,
            vmem=VM[3],
        )

        og = run(
            "out_grad",
            functools.partial(out_grad_kernel, own),
            [like((width, own), f32), like((width, own), bf16)] * 2,
            [info],
            [zp, do],
            after=[],
        )

        du, da, suffix, gtotal = run(
            "back_state",
            functools.partial(back_state_kernel, own, size),
            [blk(bf16), blk(bf16), states, state],
            [info, fac],
            dz + [attn, u, qs],
            [scratch_states],
            flops=8 * rows * size * own,
            after=[ffn_parts[0], og[0]],
        )
        after = carried(gtotal, -1)
        og_added, og_far = at.collect_far(og[2], og[3], after=[])
        og = [og[0], at.swap(og[1], 1), og_far]
        hidden_parts, hidden_sent = second_hop(hidden_outs, hidden_got, [du])
        dq, dk, dv = run(
            "back_local",
            functools.partial(back_local_kernel, own, size),
            [blk(bf16), blk(f32), blk(f32)],
            [],
            [da, v, w, q, k, plow, mask, query_decay, q0, cosine, sine],
            flops=40 * rows * rows * own,
            after=hidden_sent,
        )
        if aligned:
            ds_outs = run(
                "down_side",
                functools.partial(down_side_kernel, items, groups, block, wide, own),
                grad_outs(wide + 2 * own),
                [],
                cots + h1 + hd + [dq, du],
                flops=8 * rows * width * (wide + own),
                vmem=VM[2],
            )
        else:
            hh, cc = jnp.concatenate(h1, 0), jnp.concatenate(cots, 0)
            both = [
                mm_tn(cc, jnp.concatenate(hd, 0)),
                mm_tn(hh, dq.reshape(4 * rows, own)),
                mm_tn(hh, du.reshape(4 * rows, own)),
            ]
            ds_outs = halves(jnp.concatenate(both, 1))
        ds_got = first_hop(ds_outs)
        hidden_sums = third_hop(hidden_parts)
        grads, *part = run(
            "back_final",
            functools.partial(back_final_kernel, nw, own, size),
            [like((4, rows, 4 * own), bf16)] + two_acts,
            [info, fac],
            [suffix, after, v, ks, du, dq, dk, dv, k0, cosine, sine, key_decay] + attn_w + ffn_parts,
            flops=8 * rows * width * 4 * own,
            vmem=VM[0],
            after=[],
            alias={14 + nw + d: 1 + d for d in range(4)},
        )
        part_got1, part_got3 = at.swap(part[1], 1), at.swap(part[3], 1)
        if aligned:
            attn_outs = run(
                "attn_grad",
                functools.partial(attn_grad_kernel, items, groups, block, own),
                grad_outs(3 * own),
                [],
                h1 + [grads] + og,
                flops=6 * rows * width * 4 * own,
                vmem=VM[2],
                after=[hidden_sums[0], part_got1, part_got3],
            )
        else:
            both = [
                mm_tn(hh, grads[:, :, own : 3 * own].reshape(4 * rows, 2 * own)),
                sum(v.astype(f32) for v in og),
            ]
            attn_outs = halves(jnp.concatenate(both, 1))
        attn_got = first_hop(attn_outs)
        ds_parts, ds_sent = second_hop(ds_outs, ds_got, [attn_outs[0], hidden_sums[-1]])
        attn_parts, attn_sent = second_hop(attn_outs, attn_got, [])
        ds_sums = third_hop(ds_parts, [])
        attn_sums = third_hop(attn_parts, [])
        (both,) = run("add", add_kernel, [two_acts[1]], [], [part[2], part_got3], after=[hidden_sums[0]])
        in_sums = [part[0], part_got1, at.swap(both, 2)]
        hidden_own = scatter_split(at, info, aligned, [hidden_sums])
        (mixed,) = run(
            "mixed",
            functools.partial(mixed_kernel, kcount, kblock),
            [act()],
            [info],
            [y] + in_sums,
            [pltpu.VMEM((rows, width), f32)],
            flops=1,
            after=[],
        )
        tokens_grad = run(
            "first_back",
            functools.partial(first_back_kernel, kcount, kblock),
            [act(f32)],
            [info],
            [x, dy] + in_sums,
            [pltpu.VMEM((rows, width), f32)],
            flops=1,
        )[0]
        gg, pg = run(
            "final_hidden",
            functools.partial(final_kernel, (wide,) * 2, (hidden,) * 2),
            [like((shard, 4 * hidden), f32)] * 2,
            [info],
            hidden_own,
            flops=1,
        )
        rest_own = scatter_split(at, info, aligned, [attn_sums, ds_sums], [mixed, tokens_grad, gg])
        kg, vg, wg, ng, qg, ug = run(
            "final_rest",
            functools.partial(
                final_kernel, (own,) * 3 + (wide,) + (own,) * 2, (own,) * 3 + (hidden,) + (own,) * 2
            ),
            [like((shard, width), f32)] * 3
            + [like((shard, 4 * hidden), f32)]
            + [like((shard, width), f32)] * 2,
            [info],
            rest_own,
            after=[],
        )
        return (
            mixed.reshape(tokens.shape),
            tokens_grad.reshape(tokens.shape),
            qg,
            kg,
            vg,
            ug,
            wg,
            gg,
            pg,
            ng.T,
        )

    return body


def solution(mesh):
    items, seqs = mesh.shape["items"], mesh.shape["seq"]
    parts = jax.sharding.Mesh(mesh.devices.reshape(items, seqs // 4, 4), AXES)
    act = P("items", ("group", "member"), None)
    row = P(AXES, None)
    col = P(None, AXES)
    return jax.shard_map(
        make_body(items, seqs),
        mesh=parts,
        in_specs=(act, P()) + (row,) * 7 + (col, act),
        out_specs=(act, act) + (row,) * 7 + (col,),
        check_vma=False,
    )
```

```python
import functools
import math

import jax
import jax.numpy as jnp
from jax import lax
from jax.experimental import pallas as pl
from jax.experimental.pallas import tpu as pltpu
from jax.sharding import PartitionSpec as P

epsilon = 1e-06
AXES = ("items", "group", "member")
f32 = jnp.float32
bf16 = jnp.bfloat16
MIB = 1024 * 1024
VM = (12, 16, 16, 16)


def mm(a, b):
    return jnp.dot(a, b, preferred_element_type=f32)


def mm_tn(a, b):
    return lax.dot_general(a, b, (((0,), (0,)), ((), ())), preferred_element_type=f32)


def mm_nt(a, b):
    return lax.dot_general(a, b, (((1,), (1,)), ((), ())), preferred_element_type=f32)


def norm_factor(v):
    return lax.rsqrt(jnp.mean(v * v, axis=-1, keepdims=True) + epsilon)


def norm_back(normed, scale, grad):
    return scale * (grad - normed * jnp.mean(grad * normed, axis=-1, keepdims=True))


def like(shape, dtype):
    return jax.ShapeDtypeStruct(tuple(shape), dtype)


def run(name, kernel, outs, scalars, arrays, scratch=(), flops=0, vmem=10, after=(), alias=None):
    ins = list(scalars) + list(arrays) + list(after)
    used, held = len(scalars) + len(arrays), len(after)

    def body(*refs):
        kernel(*refs[:used], *refs[used + held :])

    size = sum(v.size * v.dtype.itemsize for v in list(arrays) + list(outs)) if flops else 0
    return pl.pallas_call(
        body,
        out_shape=list(outs),
        in_specs=[pl.BlockSpec(memory_space=pltpu.SMEM)] * len(scalars)
        + [pl.BlockSpec(memory_space=pltpu.VMEM)] * len(arrays)
        + [pl.BlockSpec(memory_space=pl.ANY)] * held,
        out_specs=[pl.BlockSpec(memory_space=pltpu.VMEM)] * len(outs),
        scratch_shapes=list(scratch),
        input_output_aliases=alias or {},
        compiler_params=pltpu.CompilerParams(vmem_limit_bytes=vmem * MIB),
        cost_estimate=pl.CostEstimate(flops=flops, bytes_accessed=size, transcendentals=0),
        name=name,
    )(*ins)


def tie(v, *after):
    anywhere = pl.BlockSpec(memory_space=pl.ANY)
    return pl.pallas_call(
        lambda *refs: None,
        out_shape=like(v.shape, v.dtype),
        in_specs=[anywhere] * (1 + len(after)),
        out_specs=anywhere,
        input_output_aliases={0: 0},
        compiler_params=pltpu.CompilerParams(vmem_limit_bytes=MIB),
        name="tie",
        cost_estimate=pl.CostEstimate(flops=0, bytes_accessed=0, transcendentals=0),
    )(v, *after)


class Place:
    def __init__(self, items, seqs):
        self.items, self.seqs, self.groups = items, seqs, seqs // 4
        self.count = items * seqs
        self.item, self.group, self.member = (lax.axis_index(name) for name in AXES)

    def swap(self, v, mask):
        return lax.ppermute(v, AXES, [(d, d ^ mask) for d in range(self.count)])

    def group_swap(self, v, k):
        return self.swap(v, 4 * k)

    def item_swap(self, v, k):
        return self.swap(v, self.seqs * k)

    def group_shift(self, v, k):
        pairs = []
        for d in range(self.count):
            g = (d % self.seqs) // 4 + k
            if 0 <= g < self.groups:
                pairs.append((d, d + 4 * k))
        return lax.ppermute(v, AXES, pairs)

    def spread(self, v):
        far = self.swap(v, 2)
        return [v, self.swap(v, 1), far, self.swap(far, 1)]

    def exchange(self, parts):
        return [parts[0]] + [self.swap(parts[d], d) for d in (1, 2, 3)]

    def collect_far(self, keep2, send3, after=()):
        pair = [keep2, self.swap(send3, 1)]
        (v,) = run("add", add_kernel, [like(keep2.shape, bf16)], [], pair, after=after)
        return v, self.swap(v, 2)

    def collect(self, keep0, send1, keep2, send3, after=()):
        far = self.collect_far(keep2, send3, after)[1]
        return [keep0, self.swap(send1, 1), far]

    def in_order(self, parts):
        out = None
        for m in (3, 2, 1, 0):
            v = jnp.concatenate([parts[m ^ k] for k in range(4)], 0)
            out = v if out is None else jnp.where(self.member == m, v, out)
        return out


def blocks_of(ref, count, size, first):
    if count == 1:
        return ref[...]
    return jnp.concatenate(
        [ref[:, pl.ds(pl.multiple_of((k ^ first) * size, size), size)] for k in range(count)], 1
    )


def rows_of(refs):
    if len(refs) == 1:
        return refs[0][...]
    return jnp.concatenate([r[...] for r in refs], 0)


def pack_kernel(own, hidden, wide, info, q, k, v, u, o, g, up, dn, *refs):
    outs, wides, small, large, sems = refs[:4], refs[4:8], refs[8], refs[9], refs[10]
    copies = [
        pltpu.make_async_copy(ref, small.at[n], sems.at[n]) for n, ref in enumerate((q, k, v, u, o))
    ] + [pltpu.make_async_copy(ref, large.at[n], sems.at[5 + n]) for n, ref in enumerate((g, up, dn))]
    for copy in copies:
        copy.start()
    for copy in copies:
        copy.wait()
    member = info[0]
    for m in range(4):

        @pl.when(member == m)
        def _():
            for d in range(4):
                j = m ^ d
                for n in range(5):
                    outs[d][:, n * own : (n + 1) * own] = small[n, :, j * own : (j + 1) * own]
                for n in range(3):
                    v = large[n, :, j * hidden : (j + 1) * hidden]
                    if wide != hidden:
                        v = jnp.concatenate(
                            [v, jnp.zeros((v.shape[0], wide - hidden), v.dtype)], 1
                        )
                    wides[d][:, n * wide : (n + 1) * wide] = v


def prep_kernel(count, block, info, x, c, h_out, c_out, scr):
    first = info[1]
    v = x[...].astype(f32)
    scr[...] = v * norm_factor(v)
    h_out[...] = blocks_of(scr, count, block, first).astype(bf16)
    scr[...] = c[...].astype(f32)
    c_out[...] = blocks_of(scr, count, block, first).astype(bf16)


def turn(v, cosine, sine):
    return v * cosine + pltpu.roll(v, v.shape[-1] // 2, 1) * sine


def project_kernel(nw, own, size, info, fac, *refs):
    h, w = refs[:4], refs[4 : 4 + nw]
    cosine, sine, qd, kd = refs[4 + nw : 8 + nw]
    q0, k0, u, v, q, k, qs, ks, prefix, total, out_w, local = refs[8 + nw :]
    member = info[0]
    out_w[...] = jnp.concatenate([r[:, 4 * own :] for r in w], 0)
    heads = own // size
    for d in range(4):
        weights = jnp.concatenate([r[:, : 4 * own] for r in w], 0)
        pre = mm(h[d][...], weights)
        q0[d] = pre[:, :own]
        k0[d] = pre[:, own : 2 * own]
        v[d] = pre[:, 2 * own : 3 * own].astype(bf16)
        u[d] = pre[:, 3 * own :]
        for n in range(heads):
            lanes = slice(n * size, (n + 1) * size)
            z = q0[d, :, lanes]
            act = turn(z * jax.nn.sigmoid(z), cosine[d], sine[d])
            q[d, :, lanes] = act.astype(bf16)
            qs[d, :, lanes] = (act * qd[n]).astype(bf16)
            z = k0[d, :, lanes]
            act = turn(z * jax.nn.sigmoid(z), cosine[d], sine[d])
            k[d, :, lanes] = act.astype(bf16)
            scaled = (act * kd[n]).astype(bf16)
            ks[d, :, lanes] = scaled
            local[member ^ d, n] = mm_tn(scaled, v[d, :, lanes])
    for n in range(heads):
        state = jnp.zeros((size, size), f32)
        for b in range(4):
            prefix[b, n] = state
            state = fac[n, 1] * state + local[b, n]
        total[n] = state


def scores_kernel(own, size, q, k, v, mask, w, intra):
    for d in range(4):
        for n in range(own // size):
            lanes = slice(n * size, (n + 1) * size)
            low = (mm_nt(q[d, :, lanes], k[d, :, lanes]) * mask[n]).astype(bf16)
            w[d, n] = low
            intra[d, :, lanes] = mm(low, v[d, :, lanes])


def attend_kernel(own, size, info, fac, prefix, before, qs, intra, u, plow, attn, *z):
    member = info[0]
    for d in range(4):
        b = member ^ d
        for n in range(own // size):
            lanes = slice(n * size, (n + 1) * size)
            low = (prefix[b, n] + fac[n, b] * before[n]).astype(bf16)
            plow[d, n] = low
            a = intra[d, :, lanes] + mm(qs[d, :, lanes], low)
            attn[d, :, lanes] = a
            z[d][:, lanes] = (a * norm_factor(a) * u[d, :, lanes]).astype(bf16)


def mid_kernel(count, block, own, info, x, *refs):
    z, o = refs[:4], refs[4:8]
    y, h2, zp, full, scr = refs[8:]
    member, first = info[0], info[1]
    for d in range(4):
        full[:, pl.ds(pl.multiple_of((member ^ d) * own, own), own)] = z[d][...]
    zp[...] = blocks_of(full, count, block, first)
    mixed = zp[...]
    for d in range(4):
        scr[:, pl.ds(pl.multiple_of((member ^ d) * own, own), own)] = mm(mixed, o[d][...])
    v = x[...].astype(f32) + scr[...]
    y[...] = v
    scr[...] = v * norm_factor(v)
    h2[...] = blocks_of(scr, count, block, first).astype(bf16)


def columns(refs, lo, hi):
    if len(refs) == 1:
        return refs[0][:, lo:hi]
    return jnp.concatenate([r[:, lo:hi] for r in refs], 0)


def columns(refs, lo, hi):
    if len(refs) == 1:
        return refs[0][:, lo:hi]
    return jnp.concatenate([r[:, lo:hi] for r in refs], 0)


def ffn_kernel(wide, h0, h1, c0, c1, *refs):
    h, c, w, outs = (h0, h1), (c0, c1), refs[:-8], refs[-8:]
    for d in range(2):
        hd, dg, df, part = outs[4 * d : 4 * d + 4]
        g = mm(h[d][...], columns(w, 0, wide))
        f = mm(h[d][...], columns(w, wide, 2 * wide))
        hd[...] = (g * f).astype(bf16)
        t = mm(c[d][...], columns(w, 2 * wide, 3 * wide))
        dg[...] = (t * f).astype(bf16)
        df[...] = (t * g).astype(bf16)
        v = mm_nt(dg[...], columns(w, 0, wide)) + mm_nt(df[...], columns(w, wide, 2 * wide))
        part[...] = v.astype(part.dtype)


def ffn_out_kernel(wide, h0, h1, h2, h3, *refs):
    w, outs = refs[:-4], refs[-4:]
    for d, h in enumerate((h0, h1, h2, h3)):
        outs[d][1] = mm_nt(h[...], columns(w, 2 * wide, 3 * wide)).astype(outs[d].dtype)


def store_grads(outs, items, groups, rows, lanes, value):
    half = groups // 2
    for part, one, two in ((0, 1, 2), (1, 2, 1)):
        send, keep2, keep0 = outs[3 * part : 3 * part + 3]
        for i in range(items):
            lo = (i * groups + part * half) * rows
            v = value[lo : lo + half * rows].astype(bf16)
            if i == 0:
                keep0[:, lanes] = v
            elif i == two:
                keep2[:, lanes] = v
            else:
                send[0 if i == one else 1, :, lanes] = v


def hidden_grad_kernel(items, groups, rows, wide, *refs):
    h, dg, df = (refs[4 * n : 4 * n + 4] for n in range(3))
    left = jnp.concatenate([r[...] for r in h], 0)
    for n, right in enumerate((dg, df)):
        value = mm_tn(left, jnp.concatenate([r[...] for r in right], 0))
        store_grads(refs[12:], items, groups, rows, slice(n * wide, (n + 1) * wide), value)


def down_side_kernel(items, groups, rows, wide, own, *refs):
    c, h, hd, dq, du, outs = refs[:4], refs[4:8], refs[8:12], refs[12], refs[13], refs[14:]
    left = jnp.concatenate([r[...] for r in c], 0)
    value = mm_tn(left, jnp.concatenate([r[...] for r in hd], 0))
    store_grads(outs, items, groups, rows, slice(0, wide), value)
    left = jnp.concatenate([r[...] for r in h], 0)
    right = jnp.concatenate([jnp.concatenate([dq[d], du[d]], 1) for d in range(4)], 0)
    store_grads(outs, items, groups, rows, slice(wide, wide + 2 * own), mm_tn(left, right))


def next_kernel(keep2, got, out):
    out[...] = (keep2[...].astype(f32) + got[1].astype(f32)).astype(bf16)


def sum_kernel(half, *refs):
    parts, outs = (refs[0:3], refs[3:6]), refs[6:]
    rows = outs[0].shape[0]
    for k, out in enumerate(outs):
        keep0, got, far = parts[k // half]
        at = slice((k % half) * rows, (k % half + 1) * rows)
        v = keep0[at].astype(f32) + got[0, at].astype(f32) + far[at].astype(f32)
        out[...] = v.astype(out.dtype)


def add_kernel(keep, got, out):
    out[...] = (keep[...] + got[...].astype(f32)).astype(bf16)


def split_kernel(pieces, info, *refs):
    outs = refs[-4:]
    member = info[0]
    rows = outs[0].shape[0]
    lo = 0
    while len(refs) > 4:
        total, away = refs[0], refs[1:pieces]
        refs = refs[pieces:]
        cols = slice(lo, lo + total.shape[1])
        lo += total.shape[1]
        for d in range(4):
            at = pl.ds(pl.multiple_of((member ^ d) * rows, rows), rows)
            v = total[at, :]
            for r in away:
                v = v + r[at, :].astype(f32)
            outs[d][:, cols] = v.astype(outs[d].dtype)


def mid_back_kernel(count, block, own, info, y, cot, a0, a1, a2, *refs):
    o = refs[:4]
    dy, do, z0, z1, z2, z3, scr = refs[4:]
    z = (z0, z1, z2, z3)
    member, first = info[0], info[1]
    scr[...] = a0[...] + a1[...].astype(f32) + a2[...].astype(f32)
    grad = blocks_of(scr, count, block, first)
    v = y[...]
    scale = norm_factor(v)
    v = cot[...].astype(f32) + norm_back(v * scale, scale, grad)
    dy[...] = v
    do[...] = v.astype(bf16)
    total = None
    for d in range(4):
        part = do[:, pl.ds(pl.multiple_of((member ^ d) * own, own), own)]
        t = mm_nt(part, o[d][...])
        total = t if total is None else total + t
    scr[...] = total
    scr[...] = blocks_of(scr, count, block, first)
    for d in range(4):
        z[d][...] = scr[:, pl.ds(pl.multiple_of((member ^ d) * own, own), own)].astype(bf16)


def out_grad_kernel(own, info, zp, do, *outs):
    member = info[0]
    left = zp[...].T
    for d in range(4):
        part = do[:, pl.ds(pl.multiple_of((member ^ d) * own, own), own)]
        outs[d][...] = mm(left, part).astype(outs[d].dtype)


def back_state_kernel(own, size, info, fac, z0, z1, z2, z3, attn, u, qs, du, da, suffix, total, local):
    member = info[0]
    z = (z0, z1, z2, z3)
    heads = own // size
    for d in range(4):
        for n in range(heads):
            lanes = slice(n * size, (n + 1) * size)
            dz = z[d][:, lanes].astype(f32)
            a = attn[d, :, lanes]
            scale = norm_factor(a)
            normed = a * scale
            du[d, :, lanes] = (dz * normed).astype(bf16)
            low = norm_back(normed, scale, dz * u[d, :, lanes]).astype(bf16)
            da[d, :, lanes] = low
            local[member ^ d, n] = mm_tn(qs[d, :, lanes], low)
    for n in range(heads):
        state = jnp.zeros((size, size), f32)
        for b in (3, 2, 1, 0):
            suffix[b, n] = state
            state = fac[n, 1] * state + local[b, n]
        total[n] = state


def back_local_kernel(own, size, da, v, w, q, k, plow, mask, qd, q0, cosine, sine, dq, dk, dv):
    for d in range(4):
        for n in range(own // size):
            lanes = slice(n * size, (n + 1) * size)
            a = da[d, :, lanes]
            ds = (mm_nt(a, v[d, :, lanes]) * mask[n]).astype(bf16)
            g = mm(ds, k[d, :, lanes]) + mm_nt(a, plow[d, n]) * qd[n]
            z = q0[d, :, lanes]
            s = jax.nn.sigmoid(z)
            g = turn(g, cosine[d], -sine[d]) * s * (1.0 + z * (1.0 - s))
            dq[d, :, lanes] = g.astype(bf16)
            dk[d, :, lanes] = mm_tn(ds, q[d, :, lanes])
            dv[d, :, lanes] = mm_tn(w[d, n], a)


def back_final_kernel(nw, own, size, info, fac, suffix, after, v, ks, du, dq, dk, dv, k0, cosine, sine, kd, *refs):
    w, outs = refs[:nw], refs[nw + 4 :]
    grads = outs[0]
    parts = outs[1:]
    member = info[0]
    for d in range(4):
        b = member ^ d
        for n in range(own // size):
            lanes = slice(n * size, (n + 1) * size)
            low = (suffix[b, n] + fac[n, 3 - b] * after[n]).astype(bf16)
            dka = dk[d, :, lanes] + mm_nt(v[d, :, lanes], low) * kd[n]
            dvv = dv[d, :, lanes] + mm(ks[d, :, lanes], low)
            z = k0[d, :, lanes]
            s = jax.nn.sigmoid(z)
            g = turn(dka, cosine[d], -sine[d]) * s * (1.0 + z * (1.0 - s))
            grads[d, :, own + n * size : own + (n + 1) * size] = g.astype(bf16)
            grads[d, :, 2 * own + n * size : 2 * own + (n + 1) * size] = dvv.astype(bf16)
        grads[d, :, :own] = dq[d]
        grads[d, :, 3 * own :] = du[d]
        weights = jnp.concatenate([r[:, : 4 * own] for r in w], 0)
        parts[d][0] = mm_nt(grads[d], weights).astype(parts[d].dtype)


def attn_grad_kernel(items, groups, rows, own, h0, h1, h2, h3, grads, o0, o1, o2, *outs):
    left = jnp.concatenate([h0[...], h1[...], h2[...], h3[...]], 0)
    value = mm_tn(left, jnp.concatenate([grads[d][:, own : 3 * own] for d in range(4)], 0))
    store_grads(outs, items, groups, rows, slice(0, 2 * own), value)
    value = o0[...].astype(f32) + o1[...].astype(f32) + o2[...].astype(f32)
    store_grads(outs, items, groups, rows, slice(2 * own, 3 * own), value)


def first_back_kernel(count, block, info, x, dy, a0, a1, a2, out, scr):
    scr[...] = a0[0] + a1[0].astype(f32) + a2[0].astype(f32)
    grad = blocks_of(scr, count, block, info[1])
    v = x[...].astype(f32)
    scale = norm_factor(v)
    out[...] = dy[...] + norm_back(v * scale, scale, grad)


def mixed_kernel(count, block, info, y, a0, a1, a2, out, scr):
    scr[...] = a0[1] + a1[1].astype(f32) + a2[1].astype(f32)
    out[...] = (y[...] + blocks_of(scr, count, block, info[1])).astype(bf16)


def final_kernel(widths, own_cols, info, p0, p1, p2, p3, *outs):
    member = info[0]
    parts = (p0, p1, p2, p3)
    for m in range(4):

        @pl.when(member == m)
        def _():
            for d in range(4):
                j = m ^ d
                lo = 0
                for out, wide, cols in zip(outs, widths, own_cols):
                    out[:, j * cols : (j + 1) * cols] = parts[d][:, lo : lo + cols].astype(f32)
                    lo += wide


def scatter_split(at, info, aligned, sums, after=()):
    if aligned:
        rows = sums[0][0].shape[0] // 4
        cols = sum(v[0].shape[1] for v in sums)
        parts = run(
            "split",
            functools.partial(split_kernel, len(sums[0])),
            [like((rows, cols), f32)] + [like((rows, cols), bf16)] * 3,
            [info],
            [v for group in sums for v in group],
            after=after,
        )
    else:
        total = jnp.concatenate([sum(v.astype(f32) for v in group) for group in sums], 1)
        rows = total.shape[0] // 4
        parts = [
            lax.dynamic_slice_in_dim(total, (at.member ^ d) * rows, rows, 0) for d in range(4)
        ]
        parts = [parts[0]] + [v.astype(bf16) for v in parts[1:]]
    return at.exchange(parts)


def rotation_tables(positions, head_size):
    half_width = head_size // 2
    pair_index = jnp.arange(half_width, dtype=jnp.int32)
    step_sizes = jnp.right_shift(jnp.full((half_width,), 8192, jnp.int32), pair_index // 5)
    phase_int = positions[:, None] * step_sizes[None, :] % 65536
    angles = phase_int.astype(f32) * (2.0 * math.pi / 65536.0)
    return (jnp.cos(angles), jnp.sin(angles))


def make_body(items, seqs):
    def body(
        tokens,
        decay_rate,
        query_weight,
        key_weight,
        value_weight,
        update_weight,
        output_weight,
        gate_weight,
        up_weight,
        down_weight,
        cotangent,
    ):
        at = Place(items, seqs)
        groups = at.groups
        width = tokens.shape[-1]
        rows = tokens.shape[1]
        heads = decay_rate.shape[0]
        size = width // heads
        own_heads = heads // 4
        own = width // 4
        shard = query_weight.shape[0]
        hidden = gate_weight.shape[1] // 4
        wide = hidden + -hidden % 256
        count, block = items * groups, 4 * shard
        first = at.item * groups + at.group
        aligned = block % 128 == 0
        if aligned:
            info = jnp.stack([at.member, first])
            kcount, kblock = count, block
        else:
            info = jnp.stack([at.member, jnp.zeros_like(first)])
            kcount, kblock = 1, width
        info = info.astype(jnp.int32)

        def arrange(pieces):
            if aligned:
                return pieces
            v = jnp.stack(pieces)
            return [v[jnp.arange(count) ^ first].reshape(width, -1)]

        def act(dtype=bf16):
            return like((rows, width), dtype)

        blk = functools.partial(like, (4, rows, own))
        x = tokens.reshape(rows, width)
        cot = cotangent.reshape(rows, width)

        half = groups // 2
        packed = pl.pallas_call(
            functools.partial(pack_kernel, own, hidden, wide),
            out_shape=[like((shard, 5 * own), bf16)] * 4 + [like((shard, 3 * wide), bf16)] * 4,
            in_specs=[pl.BlockSpec(memory_space=pltpu.SMEM)]
            + [pl.BlockSpec(memory_space=pltpu.HBM)] * 8,
            out_specs=[pl.BlockSpec(memory_space=pltpu.VMEM)] * 8,
            scratch_shapes=[
                pltpu.VMEM((5, shard, width), bf16),
                pltpu.VMEM((3, shard, 4 * hidden), bf16),
                pltpu.SemaphoreType.DMA((8,)),
            ],
            compiler_params=pltpu.CompilerParams(vmem_limit_bytes=56 * MIB),
            cost_estimate=pl.CostEstimate(flops=0, bytes_accessed=0, transcendentals=0),
            name="pack",
        )(
            info,
            query_weight,
            key_weight,
            value_weight,
            update_weight,
            output_weight,
            gate_weight,
            up_weight,
            down_weight.T,
        )
        aw = at.in_order(at.exchange(packed[:4]))
        fw = at.in_order(at.exchange(packed[4:]))
        near = [aw] + [at.group_swap(aw, k) for k in range(1, groups)]


        def sides(piece, kk):
            one, two = (1, 2) if kk < half else (2, 1)
            return {one: at.item_swap(piece, one), two: at.item_swap(piece, two)}

        def corner(got, kk, after=()):
            one, two = (1, 2) if kk < half else (2, 1)
            if after:
                got[one] = tie(got[one], *after)
            got[3] = at.item_swap(got[one], two)
            return got

        attn_p = [corner(sides(near[k], k), k) for k in range(groups)]
        h1_own, cot_own = run(
            "prep",
            functools.partial(prep_kernel, kcount, kblock),
            [act(), act()],
            [info],
            [x, cot],
            [pltpu.VMEM((rows, width), f32)],
        )
        h1_own = tie(h1_own, aw)
        h1_far = at.swap(h1_own, 2)
        fw = tie(fw, attn_p[0][1], attn_p[0][2], near[-1], h1_far)
        h1 = [h1_own, at.swap(h1_own, 1), h1_far, at.swap(h1_far, 1)]
        far_f = [fw] + [at.group_swap(fw, k) for k in range(1, groups)]
        ffn_p = [sides(far_f[k], k) for k in range(half)]
        cot_own = tie(cot_own, attn_p[-1][1], attn_p[-1][2])
        cot_far = at.swap(cot_own, 2)
        early = far_f[1:] + [v for got in ffn_p for v in got.values()]
        attn_w = arrange([near[k] if i == 0 else attn_p[k][i] for i in range(items) for k in range(groups)])
        nw = len(attn_w)

        blocks = at.group * 4 + (at.member ^ jnp.arange(4, dtype=jnp.int32))
        positions = (blocks[:, None] * rows + jnp.arange(rows, dtype=jnp.int32)).reshape(-1)
        cosine, sine = rotation_tables(positions, size)
        cosine = jnp.concatenate([cosine, cosine], 1).reshape(4, rows, size)
        sine = jnp.concatenate([-sine, sine], 1).reshape(4, rows, size)
        log_decay = lax.dynamic_slice(jnp.log(decay_rate), (at.member * own_heads,), (own_heads,))
        local = jnp.arange(rows).astype(f32)
        ld = log_decay[:, None]
        query_decay = jnp.broadcast_to(
            jnp.exp(ld * (local + 1.0))[:, :, None], (own_heads, rows, size)
        )
        key_decay = jnp.broadcast_to(
            jnp.exp(ld * (rows - 1.0 - local))[:, :, None], (own_heads, rows, size)
        )
        offset = local[:, None] - local[None, :]
        mask = jnp.where(
            offset >= 0.0, jnp.exp(log_decay[:, None, None] * jnp.maximum(offset, 0.0)), 0.0
        )
        fac = jnp.exp(ld * rows * jnp.arange(4).astype(f32))
        group_fac = jnp.exp(log_decay * (4.0 * rows))[:, None, None]

        state = like((own_heads, size, size), f32)
        states = like((4, own_heads, size, size), f32)
        states_low = like((4, own_heads, size, size), bf16)
        scratch_states = pltpu.VMEM((4, own_heads, size, size), f32)

        def carried(total, sign):
            out = at.group_shift(total, sign)
            weight = group_fac
            for k in range(2, groups):
                out = out + weight * at.group_shift(total, sign * k)
                weight = weight * group_fac
            return out

        q0, k0, u, v, q, k, qs, ks, prefix, total, out_w = run(
            "project",
            functools.partial(project_kernel, nw, own, size),
            [blk(f32), blk(f32), blk(f32)] + [blk(bf16)] * 5 + [states, state, like((width, own), bf16)],
            [info, fac],
            h1 + attn_w + [cosine, sine, query_decay, key_decay],
            [scratch_states],
            after=early,
            flops=8 * rows * width * 4 * own,
            vmem=VM[0],
        )
        before = carried(total, 1)
        out_far = at.swap(out_w, 2)
        out_core = at.swap(out_w, 1)
        w, intra = run(
            "scores",
            functools.partial(scores_kernel, own, size),
            [like((4, own_heads, rows, rows), bf16), blk(f32)],
            [],
            [q, k, v, mask],
            flops=16 * rows * rows * own,
        )
        plow, attn, *z = run(
            "attend",
            functools.partial(attend_kernel, own, size),
            [states_low, blk(f32)] + [like((rows, own), bf16)] * 4,
            [info, fac],
            [prefix, before, qs, intra, u],
            flops=8 * rows * size * own,
            after=[out_core, cot_far],
        )
        z = at.exchange(z)
        out_far = tie(out_far, attn)
        out_w = [out_w, out_core, out_far, at.swap(out_far, 1)]
        for kk in range(half, groups):
            far_f[kk] = tie(far_f[kk], prefix)
            ffn_p.append(sides(far_f[kk], kk))
        y, h2_own, zp = run(
            "mid",
            functools.partial(mid_kernel, kcount, kblock, own),
            [act(f32), act(), act()],
            [info],
            [x] + z + out_w,
            [pltpu.VMEM((rows, width), bf16), pltpu.VMEM((rows, width), f32)],
            flops=2 * rows * width * width,
            after=[v for got in ffn_p[half:] for v in got.values()],
        )
        cot_far = tie(cot_far, y)
        cots = [cot_own, at.swap(cot_own, 1), cot_far, at.swap(cot_far, 1)]
        h2 = at.spread(h2_own)
        for kk in range(groups):
            corner(ffn_p[kk], kk, [y])
        ffn_w = arrange(
            [far_f[kk] if i == 0 else ffn_p[kk][i] for i in range(items) for kk in range(groups)]
        )

        hid = like((rows, wide), bf16)
        def gated(a, b, after):
            return run(
                "ffn%d" % a,
                functools.partial(ffn_kernel, wide),
                [hid] * 3 + [act(f32)] + [hid] * 3 + [act()],
                [],
                [h2[a], h2[b], cots[a], cots[b]] + ffn_w,
                vmem=VM[1],
                after=after,
            )

        late = gated(2, 3, [])
        added, mid_far = at.collect_far(late[3], late[7])
        soon = gated(0, 1, [added])
        hd, dg, df = ([soon[n], soon[4 + n], late[n], late[4 + n]] for n in range(3))
        mid_sums = [soon[3], at.swap(soon[7], 1), mid_far]

        def item_blocks(g):
            g = g.astype(bf16).reshape(count, block, -1)[jnp.arange(count) ^ first]
            g = g.reshape(items, groups * block, -1)
            return [g[i] for i in range(items)]

        def halves(g):
            g = item_blocks(g)
            res = []
            for p, one, two in ((0, 1, 2), (1, 2, 1)):
                t = [v[p * half * block : (p + 1) * half * block] for v in g]
                res += [jnp.stack([t[one], t[3]]), t[two], t[0]]
            return res

        def grad_outs(cols):
            return [
                like((2, half * block, cols), bf16),
                like((half * block, cols), bf16),
                like((half * block, cols), bf16),
            ] * 2

        def first_hop(outs):
            return [at.item_swap(outs[0], 1), at.item_swap(outs[3], 2)]

        def second_hop(outs, got, after=()):
            res, sent = [], []
            for p, two in ((0, 2), (1, 1)):
                keep2, keep0 = outs[3 * p + 1 : 3 * p + 3]
                (v,) = run(
                    "next", next_kernel, [like(keep2.shape, bf16)], [], [keep2, got[p]], after=after
                )
                res += [keep0, got[p], at.item_swap(v, two)]
                sent.append(v)
            return res, sent

        def third_hop(parts, after=()):
            cols = parts[0].shape[1]
            res = run(
                "sum",
                functools.partial(sum_kernel, half),
                [like((block, cols), f32)] + [like((block, cols), bf16)] * (groups - 1),
                [],
                parts,
                after=after,
            )
            return [res[0]] + [at.group_swap(res[k], k) for k in range(1, groups)]

        if aligned:
            hidden_outs = run(
                "hidden_grad",
                functools.partial(hidden_grad_kernel, items, groups, block, wide),
                grad_outs(2 * wide),
                [],
                h2 + dg + df,
                vmem=VM[2],
            )
        else:
            both = [jnp.concatenate(dg, 0), jnp.concatenate(df, 0)]
            hidden_outs = halves(
                jnp.concatenate([mm_tn(jnp.concatenate(h2, 0), v) for v in both], 1)
            )
        hidden_got = first_hop(hidden_outs)

        dy, do, *dz = run(
            "mid_back",
            functools.partial(mid_back_kernel, kcount, kblock, own),
            [act(f32), act()] + [like((rows, own), bf16)] * 4,
            [info],
            [y, cot] + mid_sums + out_w,
            [pltpu.VMEM((rows, width), f32)],
            flops=2 * rows * width * width,
            after=[hidden_outs[0]],
        )
        dz = at.exchange(dz)
        two_acts = [like((2, rows, width), t) for t in (f32, bf16, f32, bf16)]
        ffn_parts = [None] * 4
        ffn_parts[:] = run(
            "ffn_out",
            functools.partial(ffn_out_kernel, wide),
            two_acts,
            [],
            hd + ffn_w,
            flops=8 * rows * width * wide,
            vmem=VM[3],
        )

        og = run(
            "out_grad",
            functools.partial(out_grad_kernel, own),
            [like((width, own), f32), like((width, own), bf16)] * 2,
            [info],
            [zp, do],
            after=[],
        )

        og_added, og_far = at.collect_far(og[2], og[3], after=[])
        og = [og[0], at.swap(og[1], 1), og_far]
        du, da, suffix, gtotal = run(
            "back_state",
            functools.partial(back_state_kernel, own, size),
            [blk(bf16), blk(bf16), states, state],
            [info, fac],
            dz + [attn, u, qs],
            [scratch_states],
            flops=8 * rows * size * own,
            after=[ffn_parts[0], og_added],
        )
        after = carried(gtotal, -1)
        hidden_parts, hidden_sent = second_hop(hidden_outs, hidden_got, [du])
        dq, dk, dv = run(
            "back_local",
            functools.partial(back_local_kernel, own, size),
            [blk(bf16), blk(f32), blk(f32)],
            [],
            [da, v, w, q, k, plow, mask, query_decay, q0, cosine, sine],
            flops=40 * rows * rows * own,
            after=hidden_sent,
        )
        if aligned:
            ds_outs = run(
                "down_side",
                functools.partial(down_side_kernel, items, groups, block, wide, own),
                grad_outs(wide + 2 * own),
                [],
                cots + h1 + hd + [dq, du],
                flops=8 * rows * width * (wide + own),
                vmem=VM[2],
            )
        else:
            hh, cc = jnp.concatenate(h1, 0), jnp.concatenate(cots, 0)
            both = [
                mm_tn(cc, jnp.concatenate(hd, 0)),
                mm_tn(hh, dq.reshape(4 * rows, own)),
                mm_tn(hh, du.reshape(4 * rows, own)),
            ]
            ds_outs = halves(jnp.concatenate(both, 1))
        ds_got = first_hop(ds_outs)
        hidden_sums = third_hop(hidden_parts)
        grads, *part = run(
            "back_final",
            functools.partial(back_final_kernel, nw, own, size),
            [like((4, rows, 4 * own), bf16)] + two_acts,
            [info, fac],
            [suffix, after, v, ks, du, dq, dk, dv, k0, cosine, sine, key_decay] + attn_w + ffn_parts,
            flops=8 * rows * width * 4 * own,
            vmem=VM[0],
            after=[hidden_sums[0], ds_outs[0], og_far],
            alias={14 + nw + d: 1 + d for d in range(4)},
        )
        part_got1, part_got3 = at.swap(part[1], 1), at.swap(part[3], 1)
        if aligned:
            attn_outs = run(
                "attn_grad",
                functools.partial(attn_grad_kernel, items, groups, block, own),
                grad_outs(3 * own),
                [],
                h1 + [grads] + og,
                flops=6 * rows * width * 4 * own,
                vmem=VM[2],
                after=[hidden_sums[0], part_got1, part_got3],
            )
        else:
            both = [
                mm_tn(hh, grads[:, :, own : 3 * own].reshape(4 * rows, 2 * own)),
                sum(v.astype(f32) for v in og),
            ]
            attn_outs = halves(jnp.concatenate(both, 1))
        attn_got = first_hop(attn_outs)
        ds_parts, ds_sent = second_hop(ds_outs, ds_got, [attn_outs[0], hidden_sums[-1]])
        attn_parts, attn_sent = second_hop(attn_outs, attn_got, [])
        ds_sums = third_hop(ds_parts, [])
        attn_sums = third_hop(attn_parts, [])
        (both,) = run("add", add_kernel, [two_acts[1]], [], [part[2], part_got3], after=[hidden_sums[0]])
        in_sums = [part[0], part_got1, at.swap(both, 2)]
        hidden_own = scatter_split(at, info, aligned, [hidden_sums])
        (mixed,) = run(
            "mixed",
            functools.partial(mixed_kernel, kcount, kblock),
            [act()],
            [info],
            [y] + in_sums,
            [pltpu.VMEM((rows, width), f32)],
            flops=1,
            after=[],
        )
        tokens_grad = run(
            "first_back",
            functools.partial(first_back_kernel, kcount, kblock),
            [act(f32)],
            [info],
            [x, dy] + in_sums,
            [pltpu.VMEM((rows, width), f32)],
            flops=1,
        )[0]
        gg, pg = run(
            "final_hidden",
            functools.partial(final_kernel, (wide,) * 2, (hidden,) * 2),
            [like((shard, 4 * hidden), f32)] * 2,
            [info],
            hidden_own,
            flops=1,
        )
        rest_own = scatter_split(at, info, aligned, [attn_sums, ds_sums], [gg, mixed])
        kg, vg, wg, ng, qg, ug = run(
            "final_rest",
            functools.partial(
                final_kernel, (own,) * 3 + (wide,) + (own,) * 2, (own,) * 3 + (hidden,) + (own,) * 2
            ),
            [like((shard, width), f32)] * 3
            + [like((shard, 4 * hidden), f32)]
            + [like((shard, width), f32)] * 2,
            [info],
            rest_own,
            after=[],
        )
        return (
            mixed.reshape(tokens.shape),
            tokens_grad.reshape(tokens.shape),
            qg,
            kg,
            vg,
            ug,
            wg,
            gg,
            pg,
            ng.T,
        )

    return body


def solution(mesh):
    items, seqs = mesh.shape["items"], mesh.shape["seq"]
    parts = jax.sharding.Mesh(mesh.devices.reshape(items, seqs // 4, 4), AXES)
    act = P("items", ("group", "member"), None)
    row = P(AXES, None)
    col = P(None, AXES)
    return jax.shard_map(
        make_body(items, seqs),
        mesh=parts,
        in_specs=(act, P()) + (row,) * 7 + (col, act),
        out_specs=(act, act) + (row,) * 7 + (col,),
        check_vma=False,
    )
```
